32 devices in a mesh: dp: 8 (over z, y), seq: 4 (over x, core).
Axes of the slice: x: 2, y: 2, z: 4, core: 2. Of those that a mesh axis runs over, the one named last changes fastest.
Arguments:
- target_in: bfloat16 [64, 512, 512], P('dp', 'seq'), may hold values from -6 to 6
- memory: bfloat16 [64, 512, 512], P('dp', 'seq'), may hold values from -6 to 6
- target_seg: int32 [64, 512], P('dp', 'seq'), may hold values from 0 to 15, never falling along the last dimension, each value on 1 to 448 neighbouring positions
- memory_seg: int32 [64, 512], P('dp', 'seq'), may hold values from 0 to 15, never falling along the last dimension, each value on 1 to 448 neighbouring positions
- self_qkv: bfloat16 [3, 512, 512], replicated, may hold values from -0.25 to 0.25
- self_bias: float32 [3, 512], replicated, may hold values from -1.5 to 1.5
- self_out: bfloat16 [512, 512], replicated, may hold values from -0.75 to 0.75
- cross_qkv: bfloat16 [3, 512, 512], replicated, may hold values from -0.25 to 0.25
- cross_bias: float32 [3, 512], replicated, may hold values from -1.5 to 1.5
- cross_out: bfloat16 [512, 512], replicated, may hold values from -0.75 to 0.75
- ffn_in: bfloat16 [512, 2048], replicated, may hold values from -0.25 to 0.25
- ffn_in_bias: float32 [2048], replicated, may hold values from -1.5 to 1.5
- ffn_out: bfloat16 [2048, 512], replicated, may hold values from -0.25 to 0.25
- ffn_out_bias: float32 [512], replicated, may hold values from -1.5 to 1.5
- norm_gain: float32 [3, 512], replicated, may hold values from 0.5 to 1.5
- norm_bias: float32 [3, 512], replicated, may hold values from -1.5 to 1.5
- cotangent: bfloat16 [64, 512, 512], P('dp', 'seq'), may hold values from -6 to 6
Outputs:
- result: bfloat16 [64, 512, 512], P('dp', 'seq')
- target_grad: bfloat16 [64, 512, 512], P('dp', 'seq')
- memory_grad: bfloat16 [64, 512, 512], P('dp', 'seq')
- self_qkv_grad: float32 [3, 512, 512], replicated
- self_bias_grad: float32 [3, 512], replicated
- self_out_grad: float32 [512, 512], replicated
- cross_qkv_grad: float32 [3, 512, 512], replicated
- cross_bias_grad: float32 [3, 512], replicated
- cross_out_grad: float32 [512, 512], replicated
- ffn_in_grad: float32 [512, 2048], replicated
- ffn_in_bias_grad: float32 [2048], replicated
- ffn_out_grad: float32 [2048, 512], replicated
- ffn_out_bias_grad: float32 [512], replicated
- norm_gain_grad: float32 [3, 512], replicated
- norm_bias_grad: float32 [3, 512], replicated
The draws below stay inside these ranges and needn't reach their ends.
Inputs may be any that keep to these rules, and one draw needn't show every extreme that they name: `target_seg`: in each row the segment numbers never fall, and each of the 16 numbers holds one or more positions; one segment of each row holds exactly 448 positions. `memory_seg`: in each row the segment numbers never fall, and each of the 16 numbers holds one or more positions; one segment of each row holds exactly 448 positions.
All inputs are finite; a program needn't handle non-finite values.
Results may differ from the reference program's by a relative error of at most 0.019.
Values may be sent and summed in bfloat16 or wider, within the bound.
No kernel may reach another device: no remote copies, remote signals or barrier semaphores. Data moves between devices by JAX's collectives and lax.ppermute only.
A program may use at most 192 MiB of HBM per device.

```python
import math
import jax
import jax.numpy as jnp
import numpy as np
from jax import lax

D = 512
HEADS = 8
HD = 64
FF = 2048
NSEG = 16
ROWS = 64
L = 512
M = 512
TMOST = 448
MMOST = 448


def levels(stream_key, dims, cuts, smallest, high):
    def one(position, shards_of):
        steps = jax.random.uniform(jax.random.fold_in(jax.random.fold_in(stream_key, 6), position), (shards_of,), jnp.float32, smallest / len(cuts), high / len(cuts))
        return jnp.repeat(jnp.exp(steps), dims[position] // shards_of).reshape((-1,) + (1,) * (len(dims) - position - 1))

    factor_of = one(*cuts[0])
    for cut in cuts[1:]:
        factor_of = factor_of * one(*cut)
    return factor_of


def profile(amount, total, limit, lean):
    loads = [(1 << 20) // math.isqrt(rank ** lean) + 1 for rank in range(2, amount + 1)]
    spare, holding = total - limit - (amount - 1), [1] * (amount - 1)
    while spare > 0:
        candidates = [i for i in range(amount - 1) if holding[i] < limit]
        pool, remaining = sum([loads[i] for i in candidates]), spare
        for i in candidates:
            extra = min(limit - holding[i], max(1, remaining * loads[i] // pool), spare)
            holding[i] = holding[i] + extra
            spare = spare - extra
    return np.array([limit] + holding)


def uneven_parts(key, number_of, total, limit, skew):
    if number_of == 2:
        one = jax.random.randint(key, (), max(1, total - limit), min(limit, total - 1) + 1)
        return jnp.stack([one, total - one])
    sizes = jnp.asarray(profile(number_of, total, limit, skew), jnp.int32)
    couples = (number_of - 1) // 2
    giver, receiver = sizes[1:1 + 2 * couples:2], sizes[2:2 + 2 * couples:2]
    slack = jnp.minimum(giver - 1, limit - receiver)
    passed = jax.random.randint(jax.random.fold_in(key, 1), (couples,), 0, 1 << 20) % (slack + 1)
    sizes = sizes.at[1:1 + 2 * couples:2].set(giver - passed).at[2:2 + 2 * couples:2].set(receiver + passed)
    return sizes[jax.random.permutation(jax.random.fold_in(key, 2), number_of)]


def gaussian(rng, dims, spread, bound, pieces=(), held_as=jnp.bfloat16):
    factor_of = levels(rng, dims, pieces, -0.22, 0.18) if pieces else 1.0
    array = jax.random.normal(rng, dims, jnp.float32) * spread * factor_of
    return jnp.minimum(jnp.maximum(array, -bound), bound).astype(held_as)


def setup_inputs(seed: int = 0) -> dict:
    splits = jax.random.split(jax.random.key(seed), 18)
    return {
        "target_in": gaussian(splits[0], (ROWS, L, D), 1.0, 6.0, ((0, 8), (1, 4))),
        "memory": gaussian(splits[1], (ROWS, M, D), 1.0, 6.0, ((0, 8), (1, 4))),
        "target_seg": jax.vmap(lambda own: jnp.searchsorted(jnp.cumsum(uneven_parts(own, NSEG, L, TMOST, 2)), jnp.arange(L), side="right"))(jax.random.split(splits[2], ROWS)).reshape((ROWS, L)).astype(jnp.int32),
        "memory_seg": jax.vmap(lambda own: jnp.searchsorted(jnp.cumsum(uneven_parts(own, NSEG, M, MMOST, 2)), jnp.arange(M), side="right"))(jax.random.split(splits[3], ROWS)).reshape((ROWS, M)).astype(jnp.int32),
        "self_qkv": gaussian(splits[4], (3, D, D), D ** -0.5, 0.25),
        "self_bias": gaussian(splits[5], (3, D), 0.3, 1.5, (), jnp.float32),
        "self_out": gaussian(splits[6], (D, D), (D // 8) ** -0.5, 0.75),
        "cross_qkv": gaussian(splits[7], (3, D, D), D ** -0.5, 0.25),
        "cross_bias": gaussian(splits[8], (3, D), 0.3, 1.5, (), jnp.float32),
        "cross_out": gaussian(splits[9], (D, D), (D // 8) ** -0.5, 0.75),
        "ffn_in": gaussian(splits[10], (D, FF), D ** -0.5, 0.25),
        "ffn_in_bias": gaussian(splits[11], (FF,), 0.3, 1.5, (), jnp.float32),
        "ffn_out": gaussian(splits[12], (FF, D), (FF // 4) ** -0.5, 0.25),
        "ffn_out_bias": gaussian(splits[13], (D,), 0.3, 1.5, (), jnp.float32),
        "norm_gain": jnp.clip(1.0 + 0.1 * jax.random.normal(splits[14], (3, D), jnp.float32), 0.5, 1.5),
        "norm_bias": gaussian(splits[15], (3, D), 0.3, 1.5, (), jnp.float32),
        "cotangent": gaussian(splits[16], (ROWS, L, D), 1.0, 6.0, ((0, 8), (1, 4))),
    }


precise = lax.Precision.HIGHEST
scale_factor = 0.125
masked_value = -1000000000.0
norm_eps = 1e-05

@jax.custom_vjp
def low(v):
    return lax.optimization_barrier(v.astype(jnp.bfloat16)).astype(jnp.float32)

@jax.custom_vjp
def low_back(v):
    return v

def low_keep(v):
    return (low(v), None)

def low_pass(kept, grad):
    return (grad,)

def back_keep(v):
    return (v, None)

def back_low(kept, grad):
    return (low(grad),)
low.defvjp(low_keep, low_pass)
low_back.defvjp(back_keep, back_low)

def matmul(first_op, second_op):
    return jnp.dot(first_op, second_op, precision=precise)

def layer_norm(hidden, gain_row, offset_row):
    center = hidden - lax.optimization_barrier(jnp.mean(hidden, axis=-1, keepdims=True))
    variance = lax.optimization_barrier(jnp.mean(center * center, axis=-1, keepdims=True))
    return center * lax.rsqrt(variance + norm_eps) * gain_row + offset_row

def attend(queries, keys_all, values_all, allowed):
    q_rows = queries.shape[0]
    k_rows = keys_all.shape[0]
    q_heads = queries.reshape(q_rows, HEADS, HD).transpose(1, 0, 2)
    k_heads = keys_all.reshape(k_rows, HEADS, HD).transpose(1, 0, 2)
    v_heads = values_all.reshape(k_rows, HEADS, HD).transpose(1, 0, 2)

    def one_head(parts):
        q_part, k_part, v_part = parts
        scores = jnp.dot(q_part, k_part.T, precision=precise) * scale_factor
        scores = low_back(jnp.where(allowed, scores, masked_value))
        top_val = lax.optimization_barrier(jnp.max(scores, axis=-1, keepdims=True))
        weights = jnp.exp(scores - top_val)
        probs = weights / lax.optimization_barrier(jnp.sum(weights, axis=-1, keepdims=True))
        return jnp.dot(low(probs), v_part, precision=precise)
    outputs = lax.map(jax.checkpoint(one_head), (q_heads, k_heads, v_heads))
    return outputs.transpose(1, 0, 2).reshape(q_rows, HEADS * HD)

def self_row(parts):
    queries, keys_all, values_all, seg_row = parts
    place = jnp.arange(seg_row.shape[0], dtype=jnp.int32)
    allowed = (seg_row[:, None] == seg_row[None, :]) & (place[:, None] >= place[None, :])
    return attend(queries, keys_all, values_all, allowed)

def cross_row(parts):
    queries, keys_all, values_all, seg_row, mem_row = parts
    allowed = seg_row[:, None] == mem_row[None, :]
    return attend(queries, keys_all, values_all, allowed)

def forward(target, source, s_qkv, s_bias, s_out, c_qkv, c_bias, c_out, w_first, b_first, w_second, b_second, gains, offsets, target_seg, memory_seg):
    target_low = low(target)
    queries = low(low_back(matmul(target_low, s_qkv[0]) + s_bias[0]))
    keys_all = low(low_back(matmul(target_low, s_qkv[1])))
    values_all = low(low_back(matmul(target_low, s_qkv[2]) + s_bias[1]))
    attended = lax.map(self_row, (queries, keys_all, values_all, target_seg))
    attended = low(low_back(attended))
    first_sum = target + low_back(matmul(attended, s_out) + s_bias[2])
    first_norm = layer_norm(first_sum, gains[0], offsets[0])
    source_low = low(source)
    c_queries = low(low_back(matmul(low(first_norm), c_qkv[0]) + c_bias[0]))
    c_keys = low(low_back(matmul(source_low, c_qkv[1])))
    c_values = low(low_back(matmul(source_low, c_qkv[2]) + c_bias[1]))
    crossed = lax.map(cross_row, (c_queries, c_keys, c_values, target_seg, memory_seg))
    crossed = low(low_back(crossed))
    second_sum = first_norm + low_back(matmul(crossed, c_out) + c_bias[2])
    second_norm = layer_norm(second_sum, gains[1], offsets[1])
    pre_act = low_back(matmul(low(second_norm), w_first) + b_first)
    activated = low(pre_act * jax.nn.sigmoid(pre_act))
    third_sum = second_norm + low_back(matmul(activated, w_second) + b_second)
    return layer_norm(third_sum, gains[2], offsets[2])

def reference(target_in, memory, target_seg, memory_seg, self_qkv, self_bias, self_out, cross_qkv, cross_bias, cross_out, ffn_in, ffn_in_bias, ffn_out, ffn_out_bias, norm_gain, norm_bias, cotangent):
    floats = tuple((item.astype(jnp.float32) for item in (target_in, memory, self_qkv, self_bias, self_out, cross_qkv, cross_bias, cross_out, ffn_in, ffn_in_bias, ffn_out, ffn_out_bias, norm_gain, norm_bias)))

    def wrapped(*values):
        return forward(*values, target_seg, memory_seg)
    output, pullback = jax.vjp(wrapped, *floats)
    grads = pullback(cotangent.astype(jnp.float32))
    return (output.astype(jnp.bfloat16), grads[0].astype(jnp.bfloat16), grads[1].astype(jnp.bfloat16), grads[2], grads[3], grads[4], grads[5], grads[6], grads[7], grads[8], grads[9], grads[10], grads[11], grads[12], grads[13])
```

```python
import functools
import jax
import jax.numpy as jnp
from jax import lax
from jax.experimental import pallas as pl
from jax.experimental.pallas import tpu as pltpu

bf16 = jnp.bfloat16
f32 = jnp.float32
BIG = 1e9
EPS = 1e-5
HD = 64


def nn(a, b):
    return jnp.dot(a, b, preferred_element_type=f32)


def nt(a, b):
    return lax.dot_general(a, b, (((1,), (1,)), ((), ())), preferred_element_type=f32)


def tn(a, b):
    return lax.dot_general(a, b, (((0,), (0,)), ((), ())), preferred_element_type=f32)


def ln_fwd(h):
    c = h - jnp.mean(h, axis=-1, keepdims=True)
    inv = lax.rsqrt(jnp.mean(c * c, axis=-1, keepdims=True) + EPS)
    return c * inv, inv


def ln_bwd(up, n, inv, gain):
    e = up * gain
    return inv * (e - jnp.mean(e, axis=-1, keepdims=True) - n * jnp.mean(e * n, axis=-1, keepdims=True))


def colsum(v):
    return jnp.sum(v.astype(f32), axis=0, keepdims=True)


def key_marks(seg_row):
    count = seg_row.shape[1]
    seg = jnp.transpose(jnp.broadcast_to(seg_row, (128, count)))
    lane = lax.broadcasted_iota(jnp.int32, (count, 128), 1)
    off = (lane.astype(f32) != seg) & (lane < 16)
    return jnp.where(off | ((lane >= 16) & (lane < 19)), 1.0, 0.0).astype(bf16)


def query_marks(seg_row):
    count = seg_row.shape[1]
    sub = lax.broadcasted_iota(jnp.int32, (16, count), 0)
    return jnp.where(sub.astype(f32) == seg_row, -BIG, 0.0).astype(bf16)


def split_rows(row):
    hi = row.astype(bf16)
    rest = row - hi.astype(f32)
    mid = rest.astype(bf16)
    low = (rest - mid.astype(f32)).astype(bf16)
    sub = lax.broadcasted_iota(jnp.int32, (16, row.shape[1]), 0)
    out = jnp.where(sub == 0, hi.astype(f32), jnp.where(sub == 1, mid.astype(f32), jnp.where(sub == 2, low.astype(f32), 0.0)))
    return out.astype(bf16)


def causal_keep(keys, queries):
    k = lax.broadcasted_iota(jnp.int32, (keys, queries), 0)
    q = lax.broadcasted_iota(jnp.int32, (keys, queries), 1)
    return k <= q


def head_rows(pair_t, which):
    z = jnp.zeros((HD, pair_t.shape[1]), bf16)
    part = pair_t[which * HD : (which + 1) * HD]
    return [part, z] if which == 0 else [z, part]


def attend_pair_fwd(q_pair, k_pair, v_pair, kmarks, qmarks, causal):
    count_q, count_k = q_pair.shape[0], k_pair.shape[0]
    qt = jnp.transpose(q_pair)
    vt = jnp.transpose(v_pair)
    lhs = jnp.concatenate([k_pair, kmarks], axis=1)
    pad = jnp.zeros((112, count_q), bf16)
    ones = jnp.ones((16, count_k), bf16)
    outs, logs = [], []
    for h in range(2):
        rhs = jnp.concatenate(head_rows(qt, h) + [qmarks, pad], axis=0)
        s = nn(lhs, rhs)
        if causal:
            s = jnp.where(causal_keep(count_k, count_q), s, -BIG)
        top = jnp.max(s, axis=0, keepdims=True)
        p = jnp.exp(s - top).astype(bf16)
        o = nn(jnp.concatenate([vt[h * HD : (h + 1) * HD], ones], axis=0), p)
        total = o[HD : HD + 1]
        outs.append((o[:HD] * (1.0 / total)).astype(bf16))
        logs.append(top + jnp.log(total))
    return jnp.concatenate(outs, axis=0), logs


def attend_pair_bwd(q_pair, k_pair, v_pair, do_pair, ot_pair, logs, kmarks, qmarks, causal):
    count_q, count_k = q_pair.shape[0], k_pair.shape[0]
    qt = jnp.transpose(q_pair)
    kt = jnp.transpose(k_pair)
    dot_ = jnp.transpose(do_pair)
    inner = dot_.astype(f32) * ot_pair.astype(f32)
    lhs_s = jnp.concatenate([k_pair, kmarks], axis=1)
    lhs_p = jnp.concatenate([v_pair, kmarks], axis=1)
    pad = jnp.zeros((96, count_q), bf16)
    z16 = jnp.zeros((16, count_q), bf16)
    lane_q = lax.broadcasted_iota(jnp.int32, (count_q, 128), 1)
    dq_t, dk, dv = [], None, None
    for h in range(2):
        rhs = jnp.concatenate(head_rows(qt, h) + [qmarks, split_rows(-logs[h]), pad], axis=0)
        s = nn(lhs_s, rhs)
        if causal:
            s = jnp.where(causal_keep(count_k, count_q), s, -BIG)
        p = jnp.exp(s)
        d = jnp.sum(inner[h * HD : (h + 1) * HD], axis=0, keepdims=True)
        rhs = jnp.concatenate(head_rows(dot_, h) + [z16, split_rows(-d), pad], axis=0)
        g = nn(lhs_p, rhs)
        ds = (p * g).astype(bf16)
        mine = (lane_q < HD) if h == 0 else (lane_q >= HD)
        zero = jnp.zeros((count_q, 128), bf16)
        v_part = nn(p.astype(bf16), jnp.where(mine, do_pair, zero))
        k_part = nn(ds, jnp.where(mine, q_pair, zero))
        dq_t.append(nn(kt[h * HD : (h + 1) * HD], ds) * 0.125)
        dv = v_part if dv is None else dv + v_part
        dk = k_part if dk is None else dk + k_part
    dq = jnp.transpose(jnp.concatenate(dq_t, axis=0).astype(bf16))
    return dq, dk.astype(bf16), dv.astype(bf16)


VMEM = pl.BlockSpec(memory_space=pltpu.VMEM)


SMEM = pl.BlockSpec(memory_space=pltpu.SMEM)


def call(body, me, ins, outs, scratch=(), limit=50 << 20, us=1, name=None):
    return pl.pallas_call(
        body,
        in_specs=[SMEM] + [VMEM] * len(ins),
        out_specs=[VMEM] * len(outs),
        out_shape=[jax.ShapeDtypeStruct(s, d) for s, d in outs],
        scratch_shapes=[pltpu.VMEM(s, d) for s, d in scratch],
        compiler_params=pltpu.CompilerParams(vmem_limit_bytes=limit),
        cost_estimate=pl.CostEstimate(flops=us * 1_000_000_000, bytes_accessed=1 << 20, transcendentals=0),
        name=name,
    )(me, *ins)


def fwd_attention(r, q_ref, k_ref, v_ref, ot_ref, log_ref, kmarks, qmarks, causal):
    for p in range(4):
        c = slice(p * 128, (p + 1) * 128)
        ot, logs = attend_pair_fwd(q_ref[r, :, c], k_ref[r, :, c], v_ref[r, :, c], kmarks, qmarks, causal)
        ot_ref[r, c, :] = ot
        for h in range(2):
            log_ref[r, p, h : h + 1, :] = logs[h]


def gather_pieces(me_ref, pieces, out_ref):
    me = me_ref[0]
    for k in range(4):
        at = pl.multiple_of((me ^ k) * 128, 128)
        out_ref[:, pl.ds(at, 128), :] = pieces[k][...]


def spread_pieces(me_ref, value_ref, pieces):
    me = me_ref[0]
    for k in range(4):
        at = pl.multiple_of((me ^ k) * 128, 128)
        for r in range(2):
            pieces[k][r] = value_ref[pl.ds(r * 512 + at, 128), :]


def self_fwd_body(me_ref, x0, x1, x2, x3, seg_ref, w_ref, b_ref, wo_ref, gain_ref, x_ref, q_ref, k_ref, v_ref, ot_ref, log_ref, n_ref, inv_ref):
    gather_pieces(me_ref, (x0, x1, x2, x3), x_ref)
    for r in range(2):
        x = x_ref[r]
        q_ref[r] = (nn(x, w_ref[0]) + b_ref[0:1]).astype(bf16) * jnp.asarray(0.125, bf16)
        k_ref[r] = nn(x, w_ref[1]).astype(bf16)
        v_ref[r] = (nn(x, w_ref[2]) + b_ref[1:2]).astype(bf16)
        seg = seg_ref[r : r + 1]
        fwd_attention(r, q_ref, k_ref, v_ref, ot_ref, log_ref, key_marks(seg), query_marks(seg), True)
        h = x.astype(f32) + tn(ot_ref[r], wo_ref[...]) + b_ref[2:3]
        n, inv = ln_fwd(h)
        n_ref[r] = n
        inv_ref[r] = jnp.broadcast_to(inv, (h.shape[0], 128))


def cross_fwd_body(me_ref, n_in_ref, m0, m1, m2, m3, seg_ref, mseg_ref, w_ref, b_ref, wo_ref, gain_ref, nb_ref, m_ref, q_ref, k_ref, v_ref, ot_ref, log_ref, n_ref, inv_ref):
    gather_pieces(me_ref, (m0, m1, m2, m3), m_ref)
    for r in range(2):
        y = n_in_ref[r] * gain_ref[0:1] + nb_ref[0:1]
        m = m_ref[r]
        q_ref[r] = (nn(y.astype(bf16), w_ref[0]) + b_ref[0:1]).astype(bf16) * jnp.asarray(0.125, bf16)
        k_ref[r] = nn(m, w_ref[1]).astype(bf16)
        v_ref[r] = (nn(m, w_ref[2]) + b_ref[1:2]).astype(bf16)
        fwd_attention(r, q_ref, k_ref, v_ref, ot_ref, log_ref, key_marks(mseg_ref[r : r + 1]), query_marks(seg_ref[r : r + 1]), False)
        h = n_in_ref[r] * gain_ref[0:1] + nb_ref[0:1] + tn(ot_ref[r], wo_ref[...]) + b_ref[2:3]
        n, inv = ln_fwd(h)
        n_ref[r] = n
        inv_ref[r] = jnp.broadcast_to(inv, (h.shape[0], 128))


def ffn_body(me_ref, n_in_ref, inv_in_ref, ot_ref, c0, c1, c2, c3, w1_ref, b1_ref, w2_ref, b2_ref, gain_ref, nb_ref, r0, r1, r2, r3, g_ref, dw1_ref, dw2_ref, dwo_ref, vec_ref, db1_ref, yb_ref, u_ref, a_ref, acc_ref, f_ref, ct_ref, res_ref):
    gather_pieces(me_ref, (c0, c1, c2, c3), ct_ref)
    FC = 512
    blocks = w1_ref.shape[1] // FC
    yb_ref[...] = (n_in_ref[...] * gain_ref[1:2] + nb_ref[1:2]).astype(bf16)
    for c in range(blocks):
        cs = slice(c * FC, (c + 1) * FC)
        u = nn(yb_ref[...], w1_ref[:, cs]) + b1_ref[:, cs]
        u_ref[:, cs] = u
        a_ref[:, cs] = (u * jax.nn.sigmoid(u)).astype(bf16)
    h = n_in_ref[...] * gain_ref[1:2] + nb_ref[1:2] + nn(a_ref[...], w2_ref[...]) + b2_ref[...]
    n, inv = ln_fwd(h)
    res_ref[...] = (n * gain_ref[2:3] + nb_ref[2:3]).astype(bf16)
    spread_pieces(me_ref, res_ref, (r0, r1, r2, r3))
    up = ct_ref[...].reshape(h.shape).astype(f32)
    vec_ref[0:1] = colsum(up * n)
    vec_ref[1:2] = colsum(up)
    g3 = ln_bwd(up, n, inv, gain_ref[2:3])
    acc_ref[...] = g3
    f3 = g3.astype(bf16)
    f_ref[...] = f3
    vec_ref[2:3] = colsum(f3)
    for c in range(blocks):
        cs = slice(c * FC, (c + 1) * FC)
        dw2_ref[cs, :] = tn(a_ref[:, cs], f_ref[...]).astype(bf16)
        da = nt(f_ref[...], w2_ref[cs, :])
        u = u_ref[:, cs]
        sg = jax.nn.sigmoid(u)
        du = (da * sg * (1.0 + u * (1.0 - sg))).astype(bf16)
        db1_ref[:, cs] = colsum(du)
        dw1_ref[cs, :] = tn(yb_ref[...], du).astype(bf16)
        acc_ref[...] += nt(du, w1_ref[:, cs])
    up = acc_ref[...]
    n = n_in_ref[...]
    vec_ref[3:4] = colsum(up * n)
    vec_ref[4:5] = colsum(up)
    g2 = ln_bwd(up, n, inv_in_ref[:, 0:1], gain_ref[1:2])
    g_ref[...] = g2
    f2 = g2.astype(bf16)
    f_ref[...] = f2
    vec_ref[5:6] = colsum(f2)
    vec_ref[6:8] = jnp.zeros((2, vec_ref.shape[1]), f32)
    for r in range(2):
        part = nn(ot_ref[r], f_ref[r * 512 : (r + 1) * 512])
        if r == 0:
            acc_ref[0:512] = part
        else:
            dwo_ref[...] = (acc_ref[0:512] + part).astype(bf16)


def bwd_attention(r, q_ref, k_ref, v_ref, do, ot_ref, log_ref, kmarks, qmarks, causal, dq_ref, dk_ref, dv_ref):
    for p in range(4):
        c = slice(p * 128, (p + 1) * 128)
        logs = [log_ref[r, p, h : h + 1, :] for h in range(2)]
        dq, dk, dv = attend_pair_bwd(q_ref[r, :, c], k_ref[r, :, c], v_ref[r, :, c], do[:, c], ot_ref[r, c, :], logs, kmarks, qmarks, causal)
        rows = slice(r * 512, (r + 1) * 512)
        dq_ref[rows, c] = dq
        dk_ref[rows, c] = dk
        dv_ref[rows, c] = dv


def cross_bwd_body(me_ref, g_ref, q_ref, k_ref, v_ref, ot_ref, log_ref, seg_ref, mseg_ref, m_ref, n1_ref, inv1_ref, ot1_ref, w_ref, wo_ref, gain_ref, nb_ref,
                   p0, p1, p2, p3, g1_ref, dw_ref, dwo_ref, vec_ref, dq_ref, dk_ref, dv_ref, do_ref, f_ref, yb_ref, mg_ref):
    for r in range(2):
        rows = slice(r * 512, (r + 1) * 512)
        do_ref[...] = nt(g_ref[rows].astype(bf16), wo_ref[...]).astype(bf16)
        bwd_attention(r, q_ref, k_ref, v_ref, do_ref[...], ot_ref, log_ref, key_marks(mseg_ref[r : r + 1]), query_marks(seg_ref[r : r + 1]), False, dq_ref, dk_ref, dv_ref)
    yb_ref[...] = (n1_ref[...] * gain_ref[0:1] + nb_ref[0:1]).astype(bf16)
    dw_ref[0] = tn(yb_ref[...], dq_ref[...]).astype(bf16)
    dw_ref[1] = tn(m_ref[...], dk_ref[...]).astype(bf16)
    dw_ref[2] = tn(m_ref[...], dv_ref[...]).astype(bf16)
    mg_ref[...] = (nt(dk_ref[...], w_ref[1]) + nt(dv_ref[...], w_ref[2])).astype(bf16)
    spread_pieces(me_ref, mg_ref, (p0, p1, p2, p3))
    vec_ref[0:1] = colsum(dq_ref[...])
    vec_ref[1:2] = colsum(dv_ref[...])
    up = g_ref[...] + nt(dq_ref[...], w_ref[0])
    n = n1_ref[...]
    vec_ref[2:3] = colsum(up * n)
    vec_ref[3:4] = colsum(up)
    g1 = ln_bwd(up, n, inv1_ref[:, 0:1], gain_ref[0:1])
    g1_ref[...] = g1
    f1 = g1.astype(bf16)
    f_ref[...] = f1
    vec_ref[4:5] = colsum(f1)
    vec_ref[5:8] = jnp.zeros((3, vec_ref.shape[1]), f32)
    dwo_ref[...] = (nn(ot1_ref[0], f_ref[0:512]) + nn(ot1_ref[1], f_ref[512:1024])).astype(bf16)


def self_bwd_body(me_ref, g_ref, q_ref, k_ref, v_ref, ot_ref, log_ref, seg_ref, x_ref, w_ref, wo_ref, p0, p1, p2, p3, dw_ref, vec_ref, dq_ref, dk_ref, dv_ref, do_ref, tg_ref):
    for r in range(2):
        rows = slice(r * 512, (r + 1) * 512)
        do_ref[...] = nt(g_ref[rows].astype(bf16), wo_ref[...]).astype(bf16)
        seg = seg_ref[r : r + 1]
        bwd_attention(r, q_ref, k_ref, v_ref, do_ref[...], ot_ref, log_ref, key_marks(seg), query_marks(seg), True, dq_ref, dk_ref, dv_ref)
    dw_ref[0] = tn(x_ref[...], dq_ref[...]).astype(bf16)
    dw_ref[1] = tn(x_ref[...], dk_ref[...]).astype(bf16)
    dw_ref[2] = tn(x_ref[...], dv_ref[...]).astype(bf16)
    tg_ref[...] = (g_ref[...] + nt(dq_ref[...], w_ref[0]) + nt(dk_ref[...], w_ref[1]) + nt(dv_ref[...], w_ref[2])).astype(bf16)
    vec_ref[0:1] = colsum(dq_ref[...])
    vec_ref[1:2] = colsum(dv_ref[...])
    spread_pieces(me_ref, tg_ref, (p0, p1, p2, p3))
    vec_ref[2:8] = jnp.zeros((6, vec_ref.shape[1]), f32)


def xor_pairs(size, mask):
    return [(i, i ^ mask) for i in range(size)]


def exchange_in(arr, me, size):
    pieces = []
    for k in range(4):
        part = lax.dynamic_slice_in_dim(arr, 2 * (me ^ k), 2, 0)
        pieces.append(lax.ppermute(part, "seq", xor_pairs(size, k)) if k else part)
    return pieces


def exchange_out(pieces, me, size):
    got = [lax.ppermute(p, "seq", xor_pairs(size, k)) if k else p for k, p in enumerate(pieces)]
    out = jnp.zeros((8,) + got[0].shape[1:], got[0].dtype)
    for k in range(4):
        out = lax.dynamic_update_slice_in_dim(out, got[k], 2 * (me ^ k), 0)
    return out


def halve(buf, axis, size, mask, bit):
    half = buf.shape[0] // 2
    send = lax.dynamic_slice_in_dim(buf, (1 - bit) * half, half, 0)
    keep = lax.dynamic_slice_in_dim(buf, bit * half, half, 0)
    return keep + lax.ppermute(send, axis, xor_pairs(size, mask))


def join(buf, axis, size, mask, bit, dtype=None):
    got = lax.ppermute(buf, axis, xor_pairs(size, mask))
    first, second = jnp.where(bit == 1, got, buf), jnp.where(bit == 1, buf, got)
    return jnp.concatenate([first, second], axis=0)


def tree_sum(buf, stages):
    for st in stages:
        buf = halve(buf, *st)
    for st in reversed(stages):
        buf = join(buf, *st)
    return buf


def butterfly(buf, stages):
    for axis, size, mask, _ in stages:
        buf = buf + lax.ppermute(buf, axis, xor_pairs(size, mask))
    return buf


def local(sizes, target_in, memory, target_seg, memory_seg, self_qkv, self_bias, self_out, cross_qkv, cross_bias, cross_out, w1, b1, w2, b2, gain, nb, cotangent):
    rows, T, D = 2, 512, 512
    N = rows * T
    FF = w1.shape[1]
    ns, nd = sizes["seq"], sizes["dp"]
    me = lax.axis_index("seq")
    dp = lax.axis_index("dp")
    mes = me.reshape(1).astype(jnp.int32)
    bits = {}
    stages = [("seq", ns, 1, me & 1)]
    m = 1
    while m < nd:
        stages.append(("dp", nd, m, (dp // m) & 1))
        m *= 2
    stages.append(("seq", ns, 2, (me >> 1) & 1))

    segs = jnp.stack([target_seg, memory_seg], axis=1)
    sp = exchange_in(segs, me, ns)
    seg4 = jnp.zeros((2, 2, 4, 128), jnp.int32)
    for k in range(4):
        seg4 = lax.dynamic_update_slice(seg4, sp[k][:, :, None, :], (0, 0, me ^ k, 0))
    seg4 = seg4.reshape(2, 2, 512).astype(f32)
    seg, mseg = seg4[:, 0], seg4[:, 1]
    act = ((rows, T, D), bf16)
    piece = [((rows, 128, D), bf16)] * 4
    xp = exchange_in(target_in, me, ns)
    xp, memory = lax.optimization_barrier((xp, memory))
    mp = exchange_in(memory, me, ns)
    mp, cotangent = lax.optimization_barrier((mp, cotangent))
    cp = exchange_in(cotangent, me, ns)
    x, qs, ks, vs, ot1, log1, n1, inv1 = call(
        self_fwd_body, mes, (*xp, seg, self_qkv, self_bias, self_out, gain),
        [act, act, act, act, ((rows, D, T), bf16), ((rows, 4, 8, T), f32), ((rows, T, D), f32), ((rows, T, 128), f32)], name="self_fwd", us=12)
    mm, qc, kc, vc, ot2, log2, n2, inv2 = call(
        cross_fwd_body, mes, (n1, *mp, seg, mseg, cross_qkv, cross_bias, cross_out, gain, nb),
        [act, act, act, act, ((rows, D, T), bf16), ((rows, 4, 8, T), f32), ((rows, T, D), f32), ((rows, T, 128), f32)], name="cross_fwd", us=14)
    n1, inv1, n2, inv2 = n1.reshape(N, D), inv1.reshape(N, 128), n2.reshape(N, D), inv2.reshape(N, 128)
    *rp, g2, dw1, dw2, dwco, vec3, db1 = call(
        ffn_body, mes, (n2, inv2, ot2, *cp, w1, b1.reshape(1, FF), w2, b2.reshape(1, D), gain, nb),
        piece + [((N, D), f32), ((FF, D), bf16), ((FF, D), bf16), ((D, D), bf16), ((8, D), f32), ((1, FF), f32)],
        [((N, D), bf16), ((N, FF), f32), ((N, FF), bf16), ((N, D), f32), ((N, D), bf16), ((rows, T, D), bf16), ((N, D), bf16)], name="ffn", us=23)
    result = exchange_out(rp, me, ns)
    ffn = tree_sum(jnp.concatenate([dw1, dw2], axis=0), stages)
    *gp, g1, dwc, dwso, vec2 = call(
        cross_bwd_body, mes, (g2, qc, kc, vc, ot2, log2, seg, mseg, mm.reshape(N, D), n1, inv1, ot1, cross_qkv, cross_out, gain, nb),
        piece + [((N, D), f32), ((3, D, D), bf16), ((D, D), bf16), ((8, D), f32)],
        [((N, D), bf16)] * 3 + [((T, D), bf16), ((N, D), bf16), ((N, D), bf16), ((N, D), bf16)], name="cross_bwd", us=22)
    mgrad = exchange_out(gp, me, ns)
    mid = tree_sum(jnp.concatenate([dwc.reshape(3 * D, D), dwso, dwco], axis=0), stages)
    *tp, dws, vec1 = call(
        self_bwd_body, mes, (g1, qs, ks, vs, ot1, log1, seg, x.reshape(N, D), self_qkv, self_out),
        piece + [((3, D, D), bf16), ((8, D), f32)],
        [((N, D), bf16)] * 3 + [((T, D), bf16), ((N, D), bf16)], name="self_bwd", us=19)
    tgrad = exchange_out(tp, me, ns)
    last = tree_sum(dws.reshape(3 * D, D), stages)
    vec = butterfly(jnp.concatenate([vec1, vec2, vec3, db1.reshape(4, D), jnp.zeros((4, D), f32)], axis=0), stages)
    v1, v2, v3, vb = vec[0:8], vec[8:16], vec[16:24], vec[24:28]
    sb = jnp.stack([v1[0], v1[1], v2[4]])
    cb = jnp.stack([v2[0], v2[1], v3[5]])
    gg = jnp.stack([v2[2], v3[3], v3[0]])
    gb = jnp.stack([v2[3], v3[4], v3[1]])
    mid = mid.astype(f32)
    dw1 = jnp.transpose(ffn[:FF].reshape(FF // D, D, D), (1, 0, 2)).reshape(D, FF).astype(f32)
    return (
        result, tgrad, mgrad,
        last.reshape(3, D, D).astype(f32), sb, mid[3 * D : 4 * D],
        mid[: 3 * D].reshape(3, D, D), cb, mid[4 * D :],
        dw1, vb.reshape(FF), ffn[FF:].astype(f32), v3[2], gg, gb,
    )


def solution(mesh):
    from jax.sharding import PartitionSpec as P

    act, seg, rep = P("dp", "seq", None), P("dp", "seq"), P()
    return jax.shard_map(
        functools.partial(local, dict(mesh.shape)),
        mesh=mesh,
        in_specs=(act, act, seg, seg) + (rep,) * 12 + (act,),
        out_specs=(act, act, act) + (rep,) * 12,
        check_vma=False,
    )
```

```python
import functools
import jax
import jax.numpy as jnp
from jax import lax
from jax.experimental import pallas as pl
from jax.experimental.pallas import tpu as pltpu

bf16 = jnp.bfloat16
f32 = jnp.float32
BIG = 1e9
EPS = 1e-5
HD = 64
FFN_TB = 512


def nn(a, b):
    return jnp.dot(a, b, preferred_element_type=f32)


def nt(a, b):
    return lax.dot_general(a, b, (((1,), (1,)), ((), ())), preferred_element_type=f32)


def tn(a, b):
    return lax.dot_general(a, b, (((0,), (0,)), ((), ())), preferred_element_type=f32)


def ln_fwd(h):
    c = h - jnp.mean(h, axis=-1, keepdims=True)
    inv = lax.rsqrt(jnp.mean(c * c, axis=-1, keepdims=True) + EPS)
    return c * inv, inv


def ln_bwd(up, n, inv, gain):
    e = up * gain
    return inv * (e - jnp.mean(e, axis=-1, keepdims=True) - n * jnp.mean(e * n, axis=-1, keepdims=True))


def colsum(v):
    return jnp.sum(v.astype(f32), axis=0, keepdims=True)


def key_marks(seg_row):
    count = seg_row.shape[1]
    seg = jnp.transpose(jnp.broadcast_to(seg_row, (128, count)))
    lane = lax.broadcasted_iota(jnp.int32, (count, 128), 1)
    off = (lane.astype(f32) != seg) & (lane < 16)
    return jnp.where(off | ((lane >= 16) & (lane < 19)), 1.0, 0.0).astype(bf16)


def query_marks(seg_row):
    count = seg_row.shape[1]
    sub = lax.broadcasted_iota(jnp.int32, (16, count), 0)
    return jnp.where(sub.astype(f32) == seg_row, -BIG, 0.0).astype(bf16)


def split_rows(row):
    hi = row.astype(bf16)
    rest = row - hi.astype(f32)
    mid = rest.astype(bf16)
    low = (rest - mid.astype(f32)).astype(bf16)
    sub = lax.broadcasted_iota(jnp.int32, (16, row.shape[1]), 0)
    out = jnp.where(sub == 0, hi.astype(f32), jnp.where(sub == 1, mid.astype(f32), jnp.where(sub == 2, low.astype(f32), 0.0)))
    return out.astype(bf16)


def causal_keep(keys, queries):
    k = lax.broadcasted_iota(jnp.int32, (keys, queries), 0)
    q = lax.broadcasted_iota(jnp.int32, (keys, queries), 1)
    return k <= q


def head_rows(pair_t, which):
    z = jnp.zeros((HD, pair_t.shape[1]), bf16)
    part = pair_t[which * HD : (which + 1) * HD]
    return [part, z] if which == 0 else [z, part]


def key_blocks(count_q, count_k, causal):
    if not causal:
        return [(0, count_k, 0)]
    half = count_k // 2
    return [(0, half, 0), (half, count_k, half)]


def masked_scores(lhs, rhs, block, causal):
    lo, hi, first = block
    s = nn(lhs[lo:hi], rhs[:, first:])
    if causal:
        size = hi - lo
        diag = jnp.where(causal_keep(size, size), s[:, :size], -BIG)
        s = diag if s.shape[1] == size else jnp.concatenate([diag, s[:, size:]], axis=1)
    return s


def attend_pair_fwd(q_pair, k_pair, v_pair, kmarks, qmarks, causal):
    count_q, count_k = q_pair.shape[0], k_pair.shape[0]
    qt = jnp.transpose(q_pair)
    vt = jnp.transpose(v_pair)
    lhs = jnp.concatenate([k_pair, kmarks], axis=1)
    pad = jnp.zeros((112, count_q), bf16)
    ones = jnp.ones((16, count_k), bf16)
    outs, logs = [], []
    for h in range(2):
        rhs = jnp.concatenate(head_rows(qt, h) + [qmarks, pad], axis=0)
        vh = jnp.concatenate([vt[h * HD : (h + 1) * HD], ones], axis=0)
        if causal:
            half = count_k // 2
            s0, s1 = (masked_scores(lhs, rhs, b, True) for b in key_blocks(count_q, count_k, True))
            top = jnp.max(s0, axis=0, keepdims=True)
            late = jnp.maximum(top[:, half:], jnp.max(s1, axis=0, keepdims=True))
            top = jnp.concatenate([top[:, :half], late], axis=1)
            o0 = nn(vh[:, :half], jnp.exp(s0 - top).astype(bf16))
            o1 = nn(vh[:, half:], jnp.exp(s1 - late).astype(bf16))
            o = jnp.concatenate([o0[:, :half], o0[:, half:] + o1], axis=1)
        else:
            s = nn(lhs, rhs)
            top = jnp.max(s, axis=0, keepdims=True)
            o = nn(vh, jnp.exp(s - top).astype(bf16))
        total = o[HD : HD + 1]
        outs.append((o[:HD] * (1.0 / total)).astype(bf16))
        logs.append(top + jnp.log(total))
    return jnp.concatenate(outs, axis=0), logs


def attend_pair_bwd(q_pair, k_pair, v_pair, do_pair, ot_pair, logs, kmarks, qmarks, causal):
    count_q, count_k = q_pair.shape[0], k_pair.shape[0]
    qt = jnp.transpose(q_pair)
    kt = jnp.transpose(k_pair)
    dot_ = jnp.transpose(do_pair)
    inner = dot_.astype(f32) * ot_pair.astype(f32)
    lhs_s = jnp.concatenate([k_pair, kmarks], axis=1)
    lhs_p = jnp.concatenate([v_pair, kmarks], axis=1)
    pad = jnp.zeros((96, count_q), bf16)
    z16 = jnp.zeros((16, count_q), bf16)
    lane_q = lax.broadcasted_iota(jnp.int32, (count_q, 128), 1)
    zero = jnp.zeros((count_q, 128), bf16)
    blocks = key_blocks(count_q, count_k, causal)
    dq_t, dk, dv = [], [None] * len(blocks), [None] * len(blocks)
    for h in range(2):
        rhs_s = jnp.concatenate(head_rows(qt, h) + [qmarks, split_rows(-logs[h]), pad], axis=0)
        d = jnp.sum(inner[h * HD : (h + 1) * HD], axis=0, keepdims=True)
        rhs_p = jnp.concatenate(head_rows(dot_, h) + [z16, split_rows(-d), pad], axis=0)
        mine = (lane_q < HD) if h == 0 else (lane_q >= HD)
        do_h, q_h = jnp.where(mine, do_pair, zero), jnp.where(mine, q_pair, zero)
        dq = None
        for i, (lo, hi, first) in enumerate(blocks):
            p = jnp.exp(masked_scores(lhs_s, rhs_s, (lo, hi, first), causal))
            g = nn(lhs_p[lo:hi], rhs_p[:, first:])
            ds = (p * g).astype(bf16)
            v_part = nn(p.astype(bf16), do_h[first:])
            k_part = nn(ds, q_h[first:])
            q_part = nn(kt[h * HD : (h + 1) * HD, lo:hi], ds)
            dq = q_part if dq is None else jnp.concatenate([dq[:, :first], dq[:, first:] + q_part], axis=1)
            dv[i] = v_part if dv[i] is None else dv[i] + v_part
            dk[i] = k_part if dk[i] is None else dk[i] + k_part
        dq_t.append(dq * 0.125)
    dq = jnp.transpose(jnp.concatenate(dq_t, axis=0).astype(bf16))
    join = lambda parts: parts[0] if len(parts) == 1 else jnp.concatenate(parts, axis=0)
    return dq, join(dk).astype(bf16), join(dv).astype(bf16)


VMEM = pl.BlockSpec(memory_space=pltpu.VMEM)
SMEM = pl.BlockSpec(memory_space=pltpu.SMEM)
ob = lax.optimization_barrier


def call(body, ins, outs, scratch=(), specs=None, grid=(), limit=50 << 20, us=1, name=None):
    return pl.pallas_call(
        body,
        grid=grid,
        in_specs=specs or [VMEM] * len(ins),
        out_specs=[VMEM] * len(outs),
        out_shape=[jax.ShapeDtypeStruct(s, d) for s, d in outs],
        scratch_shapes=[pltpu.VMEM(s, d) for s, d in scratch],
        compiler_params=pltpu.CompilerParams(vmem_limit_bytes=limit),
        cost_estimate=pl.CostEstimate(flops=us * 1_000_000_000, bytes_accessed=1 << 20, transcendentals=0),
        name=name,
    )(*ins)


def piece_start(me, k):
    return pl.multiple_of((me ^ k) * 128, 128)


def fwd_attention(q_ref, k_ref, v_ref, ot_ref, log_ref, kmarks, qmarks, causal):
    for p in range(4):
        c = slice(p * 128, (p + 1) * 128)
        ot, logs = attend_pair_fwd(q_ref[:, c], k_ref[:, c], v_ref[:, c], kmarks, qmarks, causal)
        ot_ref[c, :] = ot
        for h in range(2):
            log_ref[p, h : h + 1, :] = logs[h]


def cut_body(at_ref, x_ref, ts_ref, ms_ref, o0, o1, o2, o3):
    me = at_ref[0]
    segs = [r[...].astype(f32) for r in (ts_ref, ms_ref)]
    sub = lax.broadcasted_iota(jnp.int32, segs[0].shape, 0)
    for k, out in enumerate((o0, o1, o2, o3)):
        for r in range(2):
            row = 2 * (me ^ k) + r
            out[r, 0:128] = x_ref[row]
            line = [jnp.sum(jnp.where(sub == row, sg, 0.0), axis=0, keepdims=True) for sg in segs]
            line = jnp.concatenate(line + [jnp.zeros((1, 256), f32)], axis=1)
            out[r, 128:144] = jnp.broadcast_to(line, (16, 512)).astype(bf16)


def self_fwd_body(at_ref, x0, x1, x2, x3, w_ref, b_ref, wo_ref, x_ref, seg_ref, q_ref, k_ref, v_ref, ot_ref, log_ref, n_ref, inv_ref):
    me = at_ref[0]
    for r in range(2):
        for k, piece in enumerate((x0, x1, x2, x3)):
            at = piece_start(me, k)
            x_ref[r, pl.ds(at, 128), :] = piece[r, 0:128]
            marks = piece[r, 128:144].astype(f32)
            seg_ref[r, 0:1, pl.ds(at, 128)] = marks[0:1, 0:128]
            seg_ref[r, 1:2, pl.ds(at, 128)] = marks[0:1, 128:256]
    for r in range(2):
        x = x_ref[r]
        q_ref[r] = (nn(x, w_ref[0]) + b_ref[0:1]).astype(bf16) * jnp.asarray(0.125, bf16)
        k_ref[r] = nn(x, w_ref[1]).astype(bf16)
        v_ref[r] = (nn(x, w_ref[2]) + b_ref[1:2]).astype(bf16)
        seg = seg_ref[r, 0:1]
        fwd_attention(q_ref.at[r], k_ref.at[r], v_ref.at[r], ot_ref.at[r], log_ref.at[r], key_marks(seg), query_marks(seg), True)
        h = x_ref[r].astype(f32) + tn(ot_ref[r], wo_ref[...]) + b_ref[2:3]
        n, inv = ln_fwd(h)
        rows = slice(r * 512, (r + 1) * 512)
        n_ref[rows] = n
        inv_ref[rows] = jnp.broadcast_to(inv, (h.shape[0], 128))


def cross_fwd_body(at_ref, n1_ref, seg_ref, m0, m1, m2, m3, w_ref, b_ref, wo_ref, gain_ref, off_ref, m_ref, y_ref, q_ref, k_ref, v_ref, ot_ref, log_ref, n_ref, inv_ref):
    me = at_ref[0]
    for r in range(2):
        rows = slice(r * 512, (r + 1) * 512)
        for k, piece in enumerate((m0, m1, m2, m3)):
            m_ref[pl.ds(r * 512 + piece_start(me, k), 128), :] = piece[r]
        y_ref[rows] = (n1_ref[rows] * gain_ref[0:1] + off_ref[0:1]).astype(bf16)
        m = m_ref[rows]
        q_ref[r] = (nn(y_ref[rows], w_ref[0]) + b_ref[0:1]).astype(bf16) * jnp.asarray(0.125, bf16)
        k_ref[r] = nn(m, w_ref[1]).astype(bf16)
        v_ref[r] = (nn(m, w_ref[2]) + b_ref[1:2]).astype(bf16)
        fwd_attention(q_ref.at[r], k_ref.at[r], v_ref.at[r], ot_ref.at[r], log_ref.at[r], key_marks(seg_ref[r, 1:2]), query_marks(seg_ref[r, 0:1]), False)
        h = n1_ref[rows] * gain_ref[0:1] + off_ref[0:1] + tn(ot_ref[r], wo_ref[...]) + b_ref[2:3]
        n, inv = ln_fwd(h)
        n_ref[rows] = n
        inv_ref[rows] = jnp.broadcast_to(inv, (h.shape[0], 128))


def spread(at_ref, value_ref, pieces):
    me = at_ref[0]
    for k in range(4):
        for r in range(2):
            pieces[k][r] = value_ref[pl.ds(r * 512 + piece_start(me, k), 128), :]


def fill_rest(ref, start):
    if ref.shape[0] > start:
        ref[start:] = jnp.zeros((ref.shape[0] - start, ref.shape[1]), ref.dtype)


def ffn_body(at_ref, n_in_ref, inv_in_ref, ot_ref, c0, c1, c2, c3, w1_ref, b1_ref, w2_ref, b2_ref, gain_ref, nb_ref,
             r0, r1, r2, r3, g_ref, f2_ref, keep_ref, send_ref, vec_ref, db1_ref, yb_ref, u_ref, a_ref, du_ref, f_ref, ct_ref, res_ref):
    me, core = at_ref[0], at_ref[1]
    for k, piece in enumerate((c0, c1, c2, c3)):
        for r in range(2):
            ct_ref[pl.ds(r * 512 + piece_start(me, k), 128), :] = piece[r]
    core = at_ref[1]
    FC, TB = 512, FFN_TB
    blocks = w1_ref.shape[1] // FC
    sums = [0.0] * 6
    for t in range(n_in_ref.shape[0] // TB):
        ts = slice(t * TB, (t + 1) * TB)
        y = n_in_ref[ts] * gain_ref[1:2] + nb_ref[1:2]
        yb = y.astype(bf16)
        yb_ref[ts] = yb
        for c in range(blocks):
            cs = slice(c * FC, (c + 1) * FC)
            u = nn(yb, w1_ref[:, cs]) + b1_ref[:, cs]
            sg = 0.5 * jnp.tanh(0.5 * u) + 0.5
            u_ref[ts, cs] = (sg * (1.0 + u * (1.0 - sg)))
            a_ref[ts, cs] = (u * sg).astype(bf16)
        n, inv = ln_fwd(y + nn(a_ref[ts], w2_ref[...]) + b2_ref[...])
        res_ref[ts] = (n * gain_ref[2:3] + nb_ref[2:3]).astype(bf16)
        up = ct_ref[ts].astype(f32)
        g3 = ln_bwd(up, n, inv, gain_ref[2:3])
        f3 = g3.astype(bf16)
        f_ref[ts] = f3
        sums[0], sums[1], sums[2] = sums[0] + colsum(up * n), sums[1] + colsum(up), sums[2] + colsum(f3)
        for c in range(blocks):
            cs = slice(c * FC, (c + 1) * FC)
            du_ref[ts, cs] = (nt(f3, w2_ref[cs, :]) * u_ref[ts, cs]).astype(bf16)
        up = g3 + nt(du_ref[ts], w1_ref[...])
        n = n_in_ref[ts]
        g2 = ln_bwd(up, n, inv_in_ref[ts, 0:1], gain_ref[1:2])
        g_ref[ts] = g2
        f2 = g2.astype(bf16)
        f2_ref[ts] = f2
        sums[3], sums[4], sums[5] = sums[3] + colsum(up * n), sums[4] + colsum(up), sums[5] + colsum(f2)
    for i in range(6):
        vec_ref[i : i + 1] = sums[i]
    vec_ref[6:8] = jnp.zeros((2, vec_ref.shape[1]), f32)
    spread(at_ref, res_ref, (r0, r1, r2, r3))
    for c in range(blocks):
        block = (core * (blocks // 2) + c) % blocks
        cs = pl.ds(pl.multiple_of(block * FC, FC), FC)
        out = keep_ref if c < blocks // 2 else send_ref
        base = 2 * (c % (blocks // 2)) * FC
        out[base + FC : base + 2 * FC] = tn(a_ref[:, cs], f_ref[...]).astype(bf16)
        db1_ref[c : c + 1] = colsum(du_ref[:, cs])
        out[base : base + FC] = tn(yb_ref[...], du_ref[:, cs]).astype(bf16)
    base = blocks * FC
    for out, c in ((keep_ref, core), (send_ref, 1 - core)):
        cs = pl.ds(pl.multiple_of(c * 256, 256), 256)
        out[base : base + 256] = (nn(ot_ref[0, cs, :], f2_ref[0:512]) + nn(ot_ref[1, cs, :], f2_ref[512:1024])).astype(bf16)
        fill_rest(out, base + 256)


def attention_bwd(causal, f_ref, q_ref, k_ref, v_ref, o_ref, l_ref, seg_ref, wo_ref, dq_ref, dk_ref, dv_ref):
    for r in range(2):
        rows = slice(r * 512, (r + 1) * 512)
        do = nt(f_ref[rows], wo_ref[...]).astype(bf16)
        km = key_marks(seg_ref[r, 0:1] if causal else seg_ref[r, 1:2])
        qm = query_marks(seg_ref[r, 0:1])
        for p in range(q_ref.shape[2] // 128):
            c = slice(p * 128, (p + 1) * 128)
            logs = [l_ref[r, p, h : h + 1, :] for h in range(2)]
            dq, dk, dv = attend_pair_bwd(q_ref[r, :, c], k_ref[r, :, c], v_ref[r, :, c], do[:, c], o_ref[r, c, :], logs, km, qm, causal)
            dq_ref[rows, c] = dq
            dk_ref[rows, c] = dk
            dv_ref[rows, c] = dv


def bwd_first_body(f_ref, q_ref, k_ref, v_ref, o_ref, l_ref, seg_ref, wo_ref, dq_ref, dk_ref, dv_ref, causal):
    attention_bwd(causal, f_ref, q_ref, k_ref, v_ref, o_ref, l_ref, seg_ref, wo_ref, dq_ref, dk_ref, dv_ref)


def cross_second_body(at_ref, f_ref, q_ref, k_ref, v_ref, o_ref, l_ref, seg_ref, wo_ref, dqa, dka, dva, g_ref, n1_ref, inv1_ref, ot1_ref, w_ref, gain_ref, y_ref, m_ref,
                      p0, p1, p2, p3, g1_ref, f1_ref, keep_ref, send_ref, vec_ref, dk_ref, dv_ref, dq_ref, mg_ref):
    core = at_ref[1]
    attention_bwd(False, f_ref, q_ref, k_ref, v_ref, o_ref, l_ref, seg_ref, wo_ref, dq_ref.at[:, 256:512], dk_ref.at[:, 256:512], dv_ref.at[:, 256:512])
    for old, new in ((dqa, dq_ref), (dka, dk_ref), (dva, dv_ref)):
        new[:, 0:256] = old[...]
    mg_ref[...] = (nt(dk_ref[...], w_ref[1]) + nt(dv_ref[...], w_ref[2])).astype(bf16)
    spread(at_ref, mg_ref, (p0, p1, p2, p3))
    vec_ref[0:1] = colsum(dq_ref[...])
    vec_ref[1:2] = colsum(dv_ref[...])
    up = g_ref[...] + nt(dq_ref[...], w_ref[0])
    n = n1_ref[...]
    g1 = ln_bwd(up, n, inv1_ref[:, 0:1], gain_ref[0:1])
    g1_ref[...] = g1
    f1 = g1.astype(bf16)
    f1_ref[...] = f1
    vec_ref[2:3] = colsum(up * n)
    vec_ref[3:4] = colsum(up)
    vec_ref[4:5] = colsum(f1)
    vec_ref[5:8] = jnp.zeros((3, vec_ref.shape[1]), f32)
    for out, c in ((keep_ref, core), (send_ref, 1 - core)):
        cs = pl.ds(pl.multiple_of(c * 256, 256), 256)
        out[0:256] = tn(y_ref[:, cs], dq_ref[...]).astype(bf16)
        out[256:512] = tn(m_ref[:, cs], dk_ref[...]).astype(bf16)
        out[512:768] = tn(m_ref[:, cs], dv_ref[...]).astype(bf16)
        out[768:1024] = (nn(ot1_ref[0, cs, :], f1_ref[0:512]) + nn(ot1_ref[1, cs, :], f1_ref[512:1024])).astype(bf16)
        fill_rest(out, 1024)


def self_second_body(f_ref, q_ref, k_ref, v_ref, o_ref, l_ref, seg_ref, wo_ref, dqa, dka, dva, d_ref):
    attention_bwd(True, f_ref, q_ref, k_ref, v_ref, o_ref, l_ref, seg_ref, wo_ref, d_ref.at[0, :, 256:512], d_ref.at[1, :, 256:512], d_ref.at[2, :, 256:512])
    for j, old in enumerate((dqa, dka, dva)):
        d_ref[j, :, 0:256] = old[...]


def self_weights_body(at_ref, d_ref, x_ref, vec2_ref, vec3_ref, db1_ref, keep_ref, send_ref):
    core = at_ref[1]
    D = x_ref.shape[1]
    zero = jnp.zeros((1, D), f32)
    low = jnp.concatenate([colsum(d_ref[0]), colsum(d_ref[2])] + [zero] * 6 + [vec2_ref[...]], axis=0)
    high = jnp.concatenate([vec3_ref[...], db1_ref[...]] + [zero] * (8 - db1_ref.shape[0]), axis=0)
    pick = core == 0
    for out, c, swap in ((send_ref, 1 - core, True), (keep_ref, core, False)):
        cs = pl.ds(pl.multiple_of(c * 256, 256), 256)
        for j in range(3):
            out[j * 256 : (j + 1) * 256] = tn(x_ref[:, cs], d_ref[j]).astype(bf16)
        first, second = (high, low) if swap else (low, high)
        out[768:784] = jnp.where(pick, first, second).astype(bf16)
        fill_rest(out, 784)


def target_grad_body(at_ref, g_ref, w_ref, d_ref, p0, p1, p2, p3, tg_ref):
    tg_ref[...] = (g_ref[...] + nt(d_ref[0], w_ref[0]) + nt(d_ref[1], w_ref[1]) + nt(d_ref[2], w_ref[2])).astype(bf16)
    spread(at_ref, tg_ref, (p0, p1, p2, p3))


def xor_pairs(size, mask):
    return [(i, i ^ mask) for i in range(size)]


def advance_body(idx_ref, *refs, plan, taken):
    ins, outs = refs[:taken], refs[taken:]
    at_in, at_out = 0, 0
    for i, (kind, held, parts, lo, rows) in enumerate(plan):
        mine = ins[at_in : at_in + held]
        if kind == "sum":
            if lo:
                total = jnp.concatenate(
                    [mine[0][...].astype(f32) + mine[1][...].astype(f32), mine[2][...].astype(f32) + mine[3][...].astype(f32)], axis=0)
            else:
                total = mine[0][...].astype(f32)
                for ref in mine[1:]:
                    total = total + ref[...].astype(f32)
            if parts == 1:
                outs[at_out][...] = total.astype(bf16)
                at_out += 1
            else:
                tmp = outs[-1 - i]
                tmp[...] = total.astype(bf16)
                size = rows // parts
                for m in range(parts):
                    start = pl.multiple_of((idx_ref[i] ^ m) * size, 16)
                    outs[at_out + m][...] = tmp[pl.ds(start, size), :]
                at_out += parts
        else:
            size = rows // held
            for m in range(held):
                start = pl.multiple_of((idx_ref[i] ^ m) * size, 16)
                outs[at_out][pl.ds(start, size), :] = mine[m][...]
            at_out += 1
        at_in += held


class Chain:
    def __init__(self, dims, parity, held, rows, levels):
        self.dims, self.parity, self.held, self.lo, self.rows, self.groups = dims, parity, list(held), int(len(held) == 4), rows, levels
        self.level, self.back, self.done = -1, False, False

    def masks(self):
        out = []
        for m in range(1, 1 << len(self.groups[self.level][0])):
            both = []
            for group in self.groups[self.level]:
                md, ms = 0, 0
                for b, (axis, mask, _) in enumerate(group):
                    if m >> b & 1:
                        md, ms = (md | mask, ms) if axis == "dp" else (md, ms | mask)
                both.append((md, ms))
            out.append(both)
        return out

    def permute(self, value, both):
        nd, ns = self.dims
        pairs = []
        for d in range(nd):
            for q in range(ns):
                md, ms = both[q & 1]
                pairs.append((d * ns + q, (d ^ md) * ns + (q ^ ms)))
        return lax.ppermute(value, ("dp", "seq"), pairs)

    def index(self, level):
        idx = [jnp.int32(0), jnp.int32(0)]
        for i, group in enumerate(self.groups[level]):
            for b, st in enumerate(group):
                idx[i] = idx[i] + (st[2] << b)
        return jnp.where(self.parity == 0, idx[0], idx[1])

    def plan(self):
        if not self.back:
            last = self.level == len(self.groups) - 1
            parts = 1 if last else 1 << len(self.groups[self.level + 1][0])
            return ("sum", len(self.held), parts, self.lo, self.rows), (jnp.int32(0) if last else self.index(self.level + 1))
        return ("join", len(self.held), 1, 0, self.rows * len(self.held)), self.index(self.level)

    def landed(self, outs):
        (kind, held, parts, _, rows), _ = self.plan()
        self.lo = 0
        if kind == "sum":
            self.rows = rows // parts
            self.own, sends = outs[0], outs[1:]
            if parts == 1:
                self.back = True
                sends = [self.own] * (len(self.masks()))
            else:
                self.level += 1
        else:
            self.rows = rows
            self.own = outs[0]
            self.level -= 1
            if self.level < 0:
                self.done = True
                return
            sends = [self.own] * (len(self.masks()))
        self.sends = sends
        self.held = [self.own] + [self.permute(v, m) for v, m in zip(sends, self.masks())]


def advance(chains, name="advance"):
    chains = [c for c in chains if not c.done]
    if not chains:
        return []
    plans = [c.plan() for c in chains]
    D = chains[0].held[0].shape[1]
    ins, outs, tmp = [], [], []
    for c, (p, _) in zip(chains, plans):
        ins += c.held
        kind, held, parts, _, rows = p
        outs += [((rows // parts, D), bf16)] * parts if kind == "sum" else [((rows, D), bf16)]
        tmp.append(((rows, D) if kind == "sum" and parts > 1 else (16, D), bf16))
    idx = jnp.stack([i for _, i in plans]).astype(jnp.int32)
    got = call(functools.partial(advance_body, plan=[p for p, _ in plans], taken=len(ins)), (idx, *ins), outs, tmp[::-1],
               specs=[SMEM] + [VMEM] * len(ins), name=name)
    at, sends = 0, []
    for c, (p, _) in zip(chains, plans):
        n = p[2] if p[0] == "sum" else 1
        c.landed(got[at : at + n])
        at += n
        if not c.done:
            sends += c.sends
    return sends


def first_cut(chain):
    parts = 1 << len(chain.groups[0][0])
    size, idx = chain.rows // parts, chain.index(0)
    outs = []
    for m in range(parts):
        start = (idx ^ m) * size
        a, b = (lax.dynamic_slice_in_dim(v, start, size, 0) for v in chain.held)
        outs.append(a + b)
    chain.landed(outs)
    return chain.sends


def ordered(chains, *after):
    chains = [c for c in chains if not c.done]
    if not chains:
        return
    held = gate([c.held for c in chains], *after)
    for c, h in zip(chains, held):
        c.held = h


def core_swap(value, ns):
    return lax.ppermute(value, "seq", xor_pairs(ns, 1))


def gate(value, *deps):
    flat, tree = jax.tree.flatten(value)
    extra, _ = jax.tree.flatten(deps)
    outs = ob(tuple(flat) + tuple(extra))
    return jax.tree.unflatten(tree, outs[: len(flat)])


def exchange_in(arr, me, size):
    pieces = []
    for k in range(4):
        part = lax.dynamic_slice_in_dim(arr, 2 * (me ^ k), 2, 0)
        pieces.append(lax.ppermute(part, "seq", xor_pairs(size, k)) if k else part)
    return pieces


def exchange_out(pieces, size):
    return [lax.ppermute(p, "seq", xor_pairs(size, k)) if k else p for k, p in enumerate(pieces)]


def assemble_body(at_ref, p0, p1, p2, p3, out_ref):
    me = at_ref[0]
    for k, piece in enumerate((p0, p1, p2, p3)):
        out_ref[pl.ds(2 * (me ^ k), 2)] = piece[...]


def assemble(at, pieces):
    out = ((8,) + pieces[0].shape[1:], bf16)
    return call(assemble_body, (at, *pieces), [out], specs=[SMEM] + [VMEM] * 4, name="assemble")[0]


def final_ffn_body(at_ref, mine, other, w1_ref, w2_ref, wo_ref):
    core = at_ref[1]
    blocks = w1_ref.shape[1] // 512
    for src, c in ((mine, core), (other, 1 - core)):
        for j in range(blocks // 2):
            cs = pl.ds(pl.multiple_of((c * (blocks // 2) + j) * 512, 512), 512)
            w1_ref[:, cs] = src[2 * j * 512 : (2 * j + 1) * 512].astype(f32)
            w2_ref[cs, :] = src[(2 * j + 1) * 512 : (2 * j + 2) * 512].astype(f32)
        wo_ref[pl.ds(pl.multiple_of(c * 256, 256), 256), :] = src[blocks * 512 : blocks * 512 + 256].astype(f32)


def final_rest_body(at_ref, mine, other, c_ref, co_ref, s_ref, sb_ref, cb_ref, gg_ref, gb_ref, b1_ref, b2_ref, vec_ref):
    core = at_ref[1]
    for src, c in ((mine, core), (other, 1 - core)):
        cs = pl.ds(pl.multiple_of(c * 256, 256), 256)
        for j in range(3):
            c_ref[j, cs, :] = src[j * 256 : (j + 1) * 256].astype(f32)
            s_ref[j, cs, :] = src[1024 + j * 256 : 1024 + (j + 1) * 256].astype(f32)
        co_ref[cs, :] = src[768:1024].astype(f32)
        vec_ref[pl.ds(pl.multiple_of(c * 16, 16), 16), :] = src[1792:1808].astype(f32)
    for out, rows in ((sb_ref, (0, 1, 12)), (cb_ref, (8, 9, 21)), (gg_ref, (10, 19, 16)), (gb_ref, (11, 20, 17))):
        for i, row in enumerate(rows):
            out[i : i + 1] = vec_ref[row : row + 1]
    b2_ref[...] = vec_ref[18:19]
    b1_ref[...] = vec_ref[24 : 24 + b1_ref.shape[0]]


def local(sizes, target_in, memory, target_seg, memory_seg, self_qkv, self_bias, self_out, cross_qkv, cross_bias, cross_out, w1, b1, w2, b2, gain, nb, cotangent):
    T, D = 512, 512
    N = 2 * T
    FF = w1.shape[1]
    ns, nd = sizes["seq"], sizes["dp"]
    dims = (nd, ns)
    me = lax.axis_index("seq")
    dp = lax.axis_index("dp")
    at = jnp.stack([me, me & 1]).astype(jnp.int32)
    other = ("seq", 2, (me >> 1) & 1)
    ds = []
    m = 1
    while m < nd:
        ds.append(("dp", m, (dp // m) & 1))
        m *= 2
    core = me & 1

    def levels(even, odd, cuts=()):
        out, i = [], 0
        for n in list(cuts) + [1] * len(even):
            if i < len(even):
                out.append((even[i : i + n], odd[i : i + n]))
                i += n
        return out

    yzx, xyz = ds + [other], [other] + ds
    zyx = ds[1:2] + ds[0:1] + [other] + ds[2:]

    unit = 8 * ns * nd

    def padded(rows):
        return -(-rows // unit) * unit

    piece = [((2, 128, D), bf16)] * 4
    act2 = ((2, T, D), bf16)
    flat = ((N, D), bf16)
    saved = [((2, D, T), bf16), ((2, 4, 8, T), f32), ((N, D), f32), ((N, 128), f32)]

    xp = call(cut_body, (at, target_in, target_seg, memory_seg), [((2, 144, D), bf16)] * 4, specs=[SMEM] + [VMEM] * 3, name="cut", us=1)
    xp = exchange_out(xp, ns)
    memory = gate(memory, xp)
    mp = exchange_in(memory, me, ns)
    cotangent = gate(cotangent, mp)
    cp = exchange_in(cotangent, me, ns)
    xx, seg, qs, ks, vs, ot1, log1, n1, inv1 = call(
        self_fwd_body, (at, *xp, self_qkv, self_bias, self_out), [act2, ((2, 8, T), f32), act2, act2, act2] + saved,
        specs=[SMEM] + [VMEM] * 7, name="self_fwd", us=12)
    mm, yb, qc, kc, vc, ot2, log2, n2, inv2 = call(
        cross_fwd_body, (at, n1, seg, *mp, cross_qkv, cross_bias, cross_out, gain, nb), [flat, flat, act2, act2, act2] + saved,
        specs=[SMEM] + [VMEM] * 11, name="cross_fwd", us=14)
    h1, h2 = padded(FF + 256), 1024
    h3 = padded(1808) - h2
    *rp, g2, f2, keep, send, vec3, db1 = call(
        ffn_body, (at, n2, inv2, ot2, *cp, w1, b1.reshape(1, FF), w2, b2.reshape(1, D), gain, nb),
        piece + [((N, D), f32), flat, ((h1, D), bf16), ((h1, D), bf16), ((8, D), f32), ((FF // D, D), f32)],
        [flat, ((N, FF), f32), ((N, FF), bf16), ((N, FF), bf16), flat, flat, flat],
        specs=[SMEM] + [VMEM] * 13, name="ffn", us=23)
    got = core_swap(send, ns)

    def half_specs(p):
        cut = pl.BlockSpec((2, T, 256), lambda i: (0, 0, p))
        return [VMEM] + [cut] * 3 + [pl.BlockSpec((2, 256, T), lambda i: (0, p, 0)), pl.BlockSpec((2, 2, 8, T), lambda i: (0, p, 0, 0)), VMEM, pl.BlockSpec((256, D), lambda i: (p, 0))]

    half3 = [((N, 256), bf16)] * 3
    dca = call(functools.partial(bwd_first_body, causal=False), (f2, qc, kc, vc, ot2, log2, seg, cross_out), half3, specs=half_specs(0), grid=(1,), name="cross_bwd_a", us=10)
    dca, got = ob((dca, got))
    big = [Chain(dims, core, (keep, got), h1, levels(yzx, zyx))]
    s = first_cut(big[0])
    dca, rp = gate((dca, rp), s)
    rp = exchange_out(rp, ns)
    *gp, g1, f1, keep, send, vec2, dkc, dvc = call(
        cross_second_body, (at, f2, qc, kc, vc, ot2, log2, seg, cross_out, *dca, g2, n1, inv1, ot1, cross_qkv, gain, yb, mm),
        piece + [((N, D), f32), flat, ((h2, D), bf16), ((h2, D), bf16), ((8, D), f32), flat, flat], [flat] * 2,
        specs=[SMEM] + half_specs(1) + [VMEM] * 11, grid=(1,), name="cross_bwd_b", us=13)
    got = core_swap(send, ns)
    ordered(big, f1)
    s = advance(big)
    f1, rp = gate((f1, rp), s)
    f1, rp = ob((f1, rp))
    dsa = call(functools.partial(bwd_first_body, causal=True), (f1, qs, ks, vs, ot1, log1, seg, self_out), half3, specs=half_specs(0), grid=(1,), name="self_bwd_a", us=9)
    dsa, got = ob((dsa, got))
    ordered(big, dsa)
    s = advance(big)
    dsa, gp = gate((dsa, gp), s)
    gp = exchange_out(gp, ns)
    keep2, got2 = keep, got
    db1 = jnp.roll(db1, 2 * core, axis=0)
    dd = call(
        self_second_body, (f1, qs, ks, vs, ot1, log1, seg, self_out, *dsa), [((3, N, D), bf16)],
        specs=half_specs(1) + [VMEM] * 3, grid=(1,), name="self_bwd_b", us=7)[0]
    dd, gp = ob((dd, gp))
    ordered(big, dd)
    s = advance(big)
    keep, send = call(self_weights_body, (at, gate(dd, s), xx.reshape(N, D), vec2, vec3, db1), [((h3, D), bf16), ((h3, D), bf16)],
                      specs=[SMEM] + [VMEM] * 5, name="self_weights", us=4)
    got = core_swap(send, ns)
    rest = [Chain(dims, core, (keep2, got2, keep, got), h2 + h3, levels(yzx, xyz))]
    tp = call(target_grad_body, (at, gate(g1, send), self_qkv, dd), piece, [flat], specs=[SMEM] + [VMEM] * 3, name="target_grad", us=3)
    ordered(rest, tp)
    last = advance(rest)
    tp = exchange_out(gate(tp, last), ns)
    step = 0
    gw = None
    while not (big[0].done and rest[0].done):
        ordered(big, last)
        last = (last, advance(big)) if not big[0].done else last
        step += 1
        if step == 2:
            result, mgrad = assemble(at, gate(rp, last)), assemble(at, gate(gp, last))
            last = (last, result, mgrad)
            last = (last, tp[1], tp[2])
        if step == 3:
            tgrad = assemble(at, gate(tp, last))
            last = (last, tgrad)
        if big[0].done and gw is None:
            other_half = core_swap(gate(big[0].own, last), ns)
        ordered(rest, last)
        last = (last, advance(rest))
        if big[0].done and gw is None:
            gw = call(final_ffn_body, (at, big[0].own, gate(other_half, last)), [((D, FF), f32), ((FF, D), f32), ((D, D), f32)],
                      specs=[SMEM] + [VMEM] * 2, name="final_ffn", us=5)
            last = (last, gw)
    gw1, gw2, gwo2 = gw
    gcw, gwo1, gsw, dsb, dcb, gg, gb, gb1, gb2 = call(
        final_rest_body, (at, rest[0].own, core_swap(rest[0].own, ns)),
        [((3, D, D), f32), ((D, D), f32), ((3, D, D), f32)] + [((3, D), f32)] * 4 + [((FF // D, D), f32), ((1, D), f32)], [((32, D), f32)],
        specs=[SMEM, VMEM, VMEM], name="final_rest", us=3)
    return result, tgrad, mgrad, gsw, dsb, gwo1, gcw, dcb, gwo2, gw1, gb1.reshape(FF), gw2, gb2.reshape(D), gg, gb


def solution(mesh):
    from jax.sharding import PartitionSpec as P

    act, seg, rep = P("dp", "seq", None), P("dp", "seq"), P()
    return jax.shard_map(
        functools.partial(local, dict(mesh.shape)),
        mesh=mesh,
        in_specs=(act, act, seg, seg) + (rep,) * 12 + (act,),
        out_specs=(act, act, act) + (rep,) * 12,
        check_vma=False,
    )
```

```python
import functools
import jax
import jax.numpy as jnp
from jax import lax
from jax.experimental import pallas as pl
from jax.experimental.pallas import tpu as pltpu

bf16 = jnp.bfloat16
f32 = jnp.float32
BIG = 1e9
EPS = 1e-5
HD = 64
FFN_TB = 512


def nn(a, b):
    return jnp.dot(a, b, preferred_element_type=f32)


def nt(a, b):
    return lax.dot_general(a, b, (((1,), (1,)), ((), ())), preferred_element_type=f32)


def tn(a, b):
    return lax.dot_general(a, b, (((0,), (0,)), ((), ())), preferred_element_type=f32)


def ln_fwd(h):
    c = h - jnp.mean(h, axis=-1, keepdims=True)
    inv = lax.rsqrt(jnp.mean(c * c, axis=-1, keepdims=True) + EPS)
    return c * inv, inv


def ln_bwd(up, n, inv, gain):
    e = up * gain
    return inv * (e - jnp.mean(e, axis=-1, keepdims=True) - n * jnp.mean(e * n, axis=-1, keepdims=True))


def colsum(v):
    return jnp.sum(v.astype(f32), axis=0, keepdims=True)


def key_marks(seg_row):
    count = seg_row.shape[1]
    seg = jnp.transpose(jnp.broadcast_to(seg_row, (128, count)))
    lane = lax.broadcasted_iota(jnp.int32, (count, 128), 1)
    off = (lane.astype(f32) != seg) & (lane < 16)
    return jnp.where(off | ((lane >= 16) & (lane < 19)), 1.0, 0.0).astype(bf16)


def query_marks(seg_row):
    count = seg_row.shape[1]
    sub = lax.broadcasted_iota(jnp.int32, (16, count), 0)
    return jnp.where(sub.astype(f32) == seg_row, -BIG, 0.0).astype(bf16)


def split_rows(row):
    hi = row.astype(bf16)
    rest = row - hi.astype(f32)
    mid = rest.astype(bf16)
    low = (rest - mid.astype(f32)).astype(bf16)
    sub = lax.broadcasted_iota(jnp.int32, (16, row.shape[1]), 0)
    out = jnp.where(sub == 0, hi.astype(f32), jnp.where(sub == 1, mid.astype(f32), jnp.where(sub == 2, low.astype(f32), 0.0)))
    return out.astype(bf16)


def causal_keep(keys, queries):
    k = lax.broadcasted_iota(jnp.int32, (keys, queries), 0)
    q = lax.broadcasted_iota(jnp.int32, (keys, queries), 1)
    return k <= q


def head_rows(pair_t, which):
    z = jnp.zeros((HD, pair_t.shape[1]), bf16)
    part = pair_t[which * HD : (which + 1) * HD]
    return [part, z] if which == 0 else [z, part]


def key_blocks(count_q, count_k, causal):
    if not causal:
        return [(0, count_k, 0)]
    half = count_k // 2
    return [(0, half, 0), (half, count_k, half)]


def masked_scores(lhs, rhs, block, causal):
    lo, hi, first = block
    s = nn(lhs[lo:hi], rhs[:, first:])
    if causal:
        size = hi - lo
        diag = jnp.where(causal_keep(size, size), s[:, :size], -BIG)
        s = diag if s.shape[1] == size else jnp.concatenate([diag, s[:, size:]], axis=1)
    return s


def attend_pair_fwd(q_pair, k_pair, v_pair, kmarks, qmarks, causal):
    count_q, count_k = q_pair.shape[0], k_pair.shape[0]
    qt = jnp.transpose(q_pair)
    vt = jnp.transpose(v_pair)
    lhs = jnp.concatenate([k_pair, kmarks], axis=1)
    pad = jnp.zeros((112, count_q), bf16)
    ones = jnp.ones((16, count_k), bf16)
    outs, logs = [], []
    for h in range(2):
        rhs = jnp.concatenate(head_rows(qt, h) + [qmarks, pad], axis=0)
        vh = jnp.concatenate([vt[h * HD : (h + 1) * HD], ones], axis=0)
        if causal:
            half = count_k // 2
            s0, s1 = (masked_scores(lhs, rhs, b, True) for b in key_blocks(count_q, count_k, True))
            top = jnp.max(s0, axis=0, keepdims=True)
            late = jnp.maximum(top[:, half:], jnp.max(s1, axis=0, keepdims=True))
            top = jnp.concatenate([top[:, :half], late], axis=1)
            o0 = nn(vh[:, :half], jnp.exp(s0 - top).astype(bf16))
            o1 = nn(vh[:, half:], jnp.exp(s1 - late).astype(bf16))
            o = jnp.concatenate([o0[:, :half], o0[:, half:] + o1], axis=1)
        else:
            s = nn(lhs, rhs)
            top = jnp.max(s, axis=0, keepdims=True)
            o = nn(vh, jnp.exp(s - top).astype(bf16))
        total = o[HD : HD + 1]
        outs.append((o[:HD] * (1.0 / total)).astype(bf16))
        logs.append(top + jnp.log(total))
    return jnp.concatenate(outs, axis=0), logs


def attend_pair_bwd(q_pair, k_pair, v_pair, do_pair, ot_pair, logs, kmarks, qmarks, causal):
    count_q, count_k = q_pair.shape[0], k_pair.shape[0]
    qt = jnp.transpose(q_pair)
    kt = jnp.transpose(k_pair)
    dot_ = jnp.transpose(do_pair)
    inner = dot_.astype(f32) * ot_pair.astype(f32)
    lhs_s = jnp.concatenate([k_pair, kmarks], axis=1)
    lhs_p = jnp.concatenate([v_pair, kmarks], axis=1)
    pad = jnp.zeros((96, count_q), bf16)
    z16 = jnp.zeros((16, count_q), bf16)
    lane_q = lax.broadcasted_iota(jnp.int32, (count_q, 128), 1)
    zero = jnp.zeros((count_q, 128), bf16)
    blocks = key_blocks(count_q, count_k, causal)
    dq_t, dk, dv = [], [None] * len(blocks), [None] * len(blocks)
    for h in range(2):
        rhs_s = jnp.concatenate(head_rows(qt, h) + [qmarks, split_rows(-logs[h]), pad], axis=0)
        d = jnp.sum(inner[h * HD : (h + 1) * HD], axis=0, keepdims=True)
        rhs_p = jnp.concatenate(head_rows(dot_, h) + [z16, split_rows(-d), pad], axis=0)
        mine = (lane_q < HD) if h == 0 else (lane_q >= HD)
        do_h, q_h = jnp.where(mine, do_pair, zero), jnp.where(mine, q_pair, zero)
        dq = None
        for i, (lo, hi, first) in enumerate(blocks):
            p = jnp.exp(masked_scores(lhs_s, rhs_s, (lo, hi, first), causal))
            g = nn(lhs_p[lo:hi], rhs_p[:, first:])
            ds = (p * g).astype(bf16)
            v_part = nn(p.astype(bf16), do_h[first:])
            k_part = nn(ds, q_h[first:])
            q_part = nn(kt[h * HD : (h + 1) * HD, lo:hi], ds)
            dq = q_part if dq is None else jnp.concatenate([dq[:, :first], dq[:, first:] + q_part], axis=1)
            dv[i] = v_part if dv[i] is None else dv[i] + v_part
            dk[i] = k_part if dk[i] is None else dk[i] + k_part
        dq_t.append(dq * 0.125)
    dq = jnp.transpose(jnp.concatenate(dq_t, axis=0).astype(bf16))
    join = lambda parts: parts[0] if len(parts) == 1 else jnp.concatenate(parts, axis=0)
    return dq, join(dk).astype(bf16), join(dv).astype(bf16)


VMEM = pl.BlockSpec(memory_space=pltpu.VMEM)
SMEM = pl.BlockSpec(memory_space=pltpu.SMEM)
ob = lax.optimization_barrier


def call(body, ins, outs, scratch=(), specs=None, grid=(), limit=50 << 20, us=1, name=None):
    return pl.pallas_call(
        body,
        grid=grid,
        in_specs=specs or [VMEM] * len(ins),
        out_specs=[VMEM] * len(outs),
        out_shape=[jax.ShapeDtypeStruct(s, d) for s, d in outs],
        scratch_shapes=[pltpu.VMEM(s, d) for s, d in scratch],
        compiler_params=pltpu.CompilerParams(vmem_limit_bytes=limit),
        cost_estimate=pl.CostEstimate(flops=us * 1_000_000_000, bytes_accessed=1 << 20, transcendentals=0),
        name=name,
    )(*ins)


def piece_start(me, k):
    return pl.multiple_of((me ^ k) * 128, 128)


def fwd_attention(q_ref, k_ref, v_ref, ot_ref, log_ref, kmarks, qmarks, causal):
    for p in range(4):
        c = slice(p * 128, (p + 1) * 128)
        ot, logs = attend_pair_fwd(q_ref[:, c], k_ref[:, c], v_ref[:, c], kmarks, qmarks, causal)
        ot_ref[c, :] = ot
        for h in range(2):
            log_ref[p, h : h + 1, :] = logs[h]


def cut_body(at_ref, x_ref, ts_ref, ms_ref, o0, o1, o2, o3):
    me = at_ref[0]
    segs = [r[...].astype(f32) for r in (ts_ref, ms_ref)]
    sub = lax.broadcasted_iota(jnp.int32, segs[0].shape, 0)
    for k, out in enumerate((o0, o1, o2, o3)):
        for r in range(2):
            row = 2 * (me ^ k) + r
            out[r, 0:128] = x_ref[row]
            line = [jnp.sum(jnp.where(sub == row, sg, 0.0), axis=0, keepdims=True) for sg in segs]
            line = jnp.concatenate(line + [jnp.zeros((1, 256), f32)], axis=1)
            out[r, 128:144] = jnp.broadcast_to(line, (16, 512)).astype(bf16)


def self_fwd_body(at_ref, x0, x1, x2, x3, w_ref, b_ref, wo_ref, x_ref, seg_ref, q_ref, k_ref, v_ref, ot_ref, log_ref, n_ref, inv_ref):
    me = at_ref[0]
    for r in range(2):
        for k, piece in enumerate((x0, x1, x2, x3)):
            at = piece_start(me, k)
            x_ref[r, pl.ds(at, 128), :] = piece[r, 0:128]
            marks = piece[r, 128:144].astype(f32)
            seg_ref[r, 0:1, pl.ds(at, 128)] = marks[0:1, 0:128]
            seg_ref[r, 1:2, pl.ds(at, 128)] = marks[0:1, 128:256]
    for r in range(2):
        x = x_ref[r]
        q_ref[r] = (nn(x, w_ref[0]) + b_ref[0:1]).astype(bf16) * jnp.asarray(0.125, bf16)
        k_ref[r] = nn(x, w_ref[1]).astype(bf16)
        v_ref[r] = (nn(x, w_ref[2]) + b_ref[1:2]).astype(bf16)
        seg = seg_ref[r, 0:1]
        fwd_attention(q_ref.at[r], k_ref.at[r], v_ref.at[r], ot_ref.at[r], log_ref.at[r], key_marks(seg), query_marks(seg), True)
        h = x_ref[r].astype(f32) + tn(ot_ref[r], wo_ref[...]) + b_ref[2:3]
        n, inv = ln_fwd(h)
        rows = slice(r * 512, (r + 1) * 512)
        n_ref[rows] = n
        inv_ref[rows] = jnp.broadcast_to(inv, (h.shape[0], 128))


def cross_fwd_body(at_ref, n1_ref, seg_ref, m0, m1, m2, m3, w_ref, b_ref, wo_ref, gain_ref, off_ref, m_ref, y_ref, q_ref, k_ref, v_ref, ot_ref, log_ref, n_ref, inv_ref):
    me = at_ref[0]
    for r in range(2):
        rows = slice(r * 512, (r + 1) * 512)
        for k, piece in enumerate((m0, m1, m2, m3)):
            m_ref[pl.ds(r * 512 + piece_start(me, k), 128), :] = piece[r]
        y_ref[rows] = (n1_ref[rows] * gain_ref[0:1] + off_ref[0:1]).astype(bf16)
        m = m_ref[rows]
        q_ref[r] = (nn(y_ref[rows], w_ref[0]) + b_ref[0:1]).astype(bf16) * jnp.asarray(0.125, bf16)
        k_ref[r] = nn(m, w_ref[1]).astype(bf16)
        v_ref[r] = (nn(m, w_ref[2]) + b_ref[1:2]).astype(bf16)
        fwd_attention(q_ref.at[r], k_ref.at[r], v_ref.at[r], ot_ref.at[r], log_ref.at[r], key_marks(seg_ref[r, 1:2]), query_marks(seg_ref[r, 0:1]), False)
        h = n1_ref[rows] * gain_ref[0:1] + off_ref[0:1] + tn(ot_ref[r], wo_ref[...]) + b_ref[2:3]
        n, inv = ln_fwd(h)
        n_ref[rows] = n
        inv_ref[rows] = jnp.broadcast_to(inv, (h.shape[0], 128))


def spread(at_ref, value_ref, pieces):
    me = at_ref[0]
    for k in range(4):
        for r in range(2):
            pieces[k][r] = value_ref[pl.ds(r * 512 + piece_start(me, k), 128), :]


def fill_rest(ref, start):
    if ref.shape[0] > start:
        ref[start:] = jnp.zeros((ref.shape[0] - start, ref.shape[1]), ref.dtype)


def ffn_body(at_ref, n_in_ref, inv_in_ref, ot_ref, c0, c1, c2, c3, w1_ref, b1_ref, w2_ref, b2_ref, gain_ref, nb_ref,
             r0, r1, r2, r3, g_ref, f2_ref, keep_ref, send_ref, vec_ref, db1_ref, yb_ref, u_ref, a_ref, du_ref, f_ref, ct_ref, res_ref):
    me, core = at_ref[0], at_ref[1]
    for k, piece in enumerate((c0, c1, c2, c3)):
        for r in range(2):
            ct_ref[pl.ds(r * 512 + piece_start(me, k), 128), :] = piece[r]
    core = at_ref[1]
    FC, TB = 512, FFN_TB
    blocks = w1_ref.shape[1] // FC
    sums = [0.0] * 6
    for t in range(n_in_ref.shape[0] // TB):
        ts = slice(t * TB, (t + 1) * TB)
        y = n_in_ref[ts] * gain_ref[1:2] + nb_ref[1:2]
        yb = y.astype(bf16)
        yb_ref[ts] = yb
        for c in range(blocks):
            cs = slice(c * FC, (c + 1) * FC)
            u = nn(yb, w1_ref[:, cs]) + b1_ref[:, cs]
            sg = 0.5 * jnp.tanh(0.5 * u) + 0.5
            u_ref[ts, cs] = (sg * (1.0 + u * (1.0 - sg)))
            a_ref[ts, cs] = (u * sg).astype(bf16)
        n, inv = ln_fwd(y + nn(a_ref[ts], w2_ref[...]) + b2_ref[...])
        res_ref[ts] = (n * gain_ref[2:3] + nb_ref[2:3]).astype(bf16)
        up = ct_ref[ts].astype(f32)
        g3 = ln_bwd(up, n, inv, gain_ref[2:3])
        f3 = g3.astype(bf16)
        f_ref[ts] = f3
        sums[0], sums[1], sums[2] = sums[0] + colsum(up * n), sums[1] + colsum(up), sums[2] + colsum(f3)
        for c in range(blocks):
            cs = slice(c * FC, (c + 1) * FC)
            du_ref[ts, cs] = (nt(f3, w2_ref[cs, :]) * u_ref[ts, cs]).astype(bf16)
        up = g3 + nt(du_ref[ts], w1_ref[...])
        n = n_in_ref[ts]
        g2 = ln_bwd(up, n, inv_in_ref[ts, 0:1], gain_ref[1:2])
        g_ref[ts] = g2
        f2 = g2.astype(bf16)
        f2_ref[ts] = f2
        sums[3], sums[4], sums[5] = sums[3] + colsum(up * n), sums[4] + colsum(up), sums[5] + colsum(f2)
    for i in range(6):
        vec_ref[i : i + 1] = sums[i]
    vec_ref[6:8] = jnp.zeros((2, vec_ref.shape[1]), f32)
    spread(at_ref, res_ref, (r0, r1, r2, r3))
    for c in range(blocks):
        block = (core * (blocks // 2) + c) % blocks
        cs = pl.ds(pl.multiple_of(block * FC, FC), FC)
        out = keep_ref if c < blocks // 2 else send_ref
        base = 2 * (c % (blocks // 2)) * FC
        out[base + FC : base + 2 * FC] = tn(a_ref[:, cs], f_ref[...]).astype(bf16)
        db1_ref[c : c + 1] = colsum(du_ref[:, cs])
        out[base : base + FC] = tn(yb_ref[...], du_ref[:, cs]).astype(bf16)
    base = blocks * FC
    for out, c in ((keep_ref, core), (send_ref, 1 - core)):
        cs = pl.ds(pl.multiple_of(c * 256, 256), 256)
        out[base : base + 256] = (nn(ot_ref[0, cs, :], f2_ref[0:512]) + nn(ot_ref[1, cs, :], f2_ref[512:1024])).astype(bf16)
        fill_rest(out, base + 256)


def attention_bwd(causal, f_ref, q_ref, k_ref, v_ref, o_ref, l_ref, seg_ref, wo_ref, dq_ref, dk_ref, dv_ref):
    for r in range(2):
        rows = slice(r * 512, (r + 1) * 512)
        do = nt(f_ref[rows], wo_ref[...]).astype(bf16)
        km = key_marks(seg_ref[r, 0:1] if causal else seg_ref[r, 1:2])
        qm = query_marks(seg_ref[r, 0:1])
        for p in range(q_ref.shape[2] // 128):
            c = slice(p * 128, (p + 1) * 128)
            logs = [l_ref[r, p, h : h + 1, :] for h in range(2)]
            dq, dk, dv = attend_pair_bwd(q_ref[r, :, c], k_ref[r, :, c], v_ref[r, :, c], do[:, c], o_ref[r, c, :], logs, km, qm, causal)
            dq_ref[rows, c] = dq
            dk_ref[rows, c] = dk
            dv_ref[rows, c] = dv


def bwd_first_body(f_ref, q_ref, k_ref, v_ref, o_ref, l_ref, seg_ref, wo_ref, dq_ref, dk_ref, dv_ref, causal):
    attention_bwd(causal, f_ref, q_ref, k_ref, v_ref, o_ref, l_ref, seg_ref, wo_ref, dq_ref, dk_ref, dv_ref)


def cross_second_body(at_ref, f_ref, q_ref, k_ref, v_ref, o_ref, l_ref, seg_ref, wo_ref, dqa, dka, dva, g_ref, n1_ref, inv1_ref, ot1_ref, w_ref, gain_ref, y_ref, m_ref,
                      p0, p1, p2, p3, g1_ref, f1_ref, keep_ref, send_ref, vec_ref, dk_ref, dv_ref, dq_ref, mg_ref):
    core = at_ref[1]
    attention_bwd(False, f_ref, q_ref, k_ref, v_ref, o_ref, l_ref, seg_ref, wo_ref, dq_ref.at[:, 256:512], dk_ref.at[:, 256:512], dv_ref.at[:, 256:512])
    for old, new in ((dqa, dq_ref), (dka, dk_ref), (dva, dv_ref)):
        new[:, 0:256] = old[...]
    mg_ref[...] = (nt(dk_ref[...], w_ref[1]) + nt(dv_ref[...], w_ref[2])).astype(bf16)
    spread(at_ref, mg_ref, (p0, p1, p2, p3))
    vec_ref[0:1] = colsum(dq_ref[...])
    vec_ref[1:2] = colsum(dv_ref[...])
    up = g_ref[...] + nt(dq_ref[...], w_ref[0])
    n = n1_ref[...]
    g1 = ln_bwd(up, n, inv1_ref[:, 0:1], gain_ref[0:1])
    g1_ref[...] = g1
    f1 = g1.astype(bf16)
    f1_ref[...] = f1
    vec_ref[2:3] = colsum(up * n)
    vec_ref[3:4] = colsum(up)
    vec_ref[4:5] = colsum(f1)
    vec_ref[5:8] = jnp.zeros((3, vec_ref.shape[1]), f32)
    for out, c in ((keep_ref, core), (send_ref, 1 - core)):
        cs = pl.ds(pl.multiple_of(c * 256, 256), 256)
        out[0:256] = tn(y_ref[:, cs], dq_ref[...]).astype(bf16)
        out[256:512] = tn(m_ref[:, cs], dk_ref[...]).astype(bf16)
        out[512:768] = tn(m_ref[:, cs], dv_ref[...]).astype(bf16)
        out[768:1024] = (nn(ot1_ref[0, cs, :], f1_ref[0:512]) + nn(ot1_ref[1, cs, :], f1_ref[512:1024])).astype(bf16)
        fill_rest(out, 1024)


def self_second_body(f_ref, q_ref, k_ref, v_ref, o_ref, l_ref, seg_ref, wo_ref, dqa, dka, dva, d_ref):
    attention_bwd(True, f_ref, q_ref, k_ref, v_ref, o_ref, l_ref, seg_ref, wo_ref, d_ref.at[0, :, 256:512], d_ref.at[1, :, 256:512], d_ref.at[2, :, 256:512])
    for j, old in enumerate((dqa, dka, dva)):
        d_ref[j, :, 0:256] = old[...]


def self_weights_body(at_ref, d_ref, x_ref, vec2_ref, vec3_ref, db1_ref, keep_ref, send_ref):
    core = at_ref[1]
    D = x_ref.shape[1]
    zero = jnp.zeros((1, D), f32)
    low = jnp.concatenate([colsum(d_ref[0]), colsum(d_ref[2])] + [zero] * 6 + [vec2_ref[...]], axis=0)
    high = jnp.concatenate([vec3_ref[...], db1_ref[...]] + [zero] * (8 - db1_ref.shape[0]), axis=0)
    pick = core == 0
    for out, c, swap in ((send_ref, 1 - core, True), (keep_ref, core, False)):
        cs = pl.ds(pl.multiple_of(c * 256, 256), 256)
        for j in range(3):
            out[j * 256 : (j + 1) * 256] = tn(x_ref[:, cs], d_ref[j]).astype(bf16)
        first, second = (high, low) if swap else (low, high)
        out[768:784] = jnp.where(pick, first, second).astype(bf16)
        fill_rest(out, 784)


def target_grad_body(at_ref, g_ref, w_ref, d_ref, p0, p1, p2, p3, tg_ref):
    tg_ref[...] = (g_ref[...] + nt(d_ref[0], w_ref[0]) + nt(d_ref[1], w_ref[1]) + nt(d_ref[2], w_ref[2])).astype(bf16)
    spread(at_ref, tg_ref, (p0, p1, p2, p3))


def xor_pairs(size, mask):
    return [(i, i ^ mask) for i in range(size)]


def advance_body(idx_ref, *refs, plan, taken):
    ins, outs = refs[:taken], refs[taken:]
    at_in, at_out = 0, 0
    for i, (kind, held, parts, lo, rows) in enumerate(plan):
        mine = ins[at_in : at_in + held]
        if kind == "sum":
            if lo:
                total = jnp.concatenate(
                    [mine[0][...].astype(f32) + mine[1][...].astype(f32), mine[2][...].astype(f32) + mine[3][...].astype(f32)], axis=0)
            else:
                total = mine[0][...].astype(f32)
                for ref in mine[1:]:
                    total = total + ref[...].astype(f32)
            if parts == 1:
                outs[at_out][...] = total.astype(bf16)
                at_out += 1
            else:
                tmp = outs[-1 - i]
                tmp[...] = total.astype(bf16)
                size = rows // parts
                for m in range(parts):
                    start = pl.multiple_of((idx_ref[i] ^ m) * size, 16)
                    outs[at_out + m][...] = tmp[pl.ds(start, size), :]
                at_out += parts
        else:
            size = rows // held
            for m in range(held):
                start = pl.multiple_of((idx_ref[i] ^ m) * size, 16)
                outs[at_out][pl.ds(start, size), :] = mine[m][...]
            at_out += 1
        at_in += held


class Chain:
    def __init__(self, dims, parity, held, rows, levels):
        self.dims, self.parity, self.held, self.lo, self.rows, self.groups = dims, parity, list(held), int(len(held) == 4), rows, levels
        self.level, self.back, self.done = -1, False, False

    def masks(self):
        out = []
        for m in range(1, 1 << len(self.groups[self.level][0])):
            both = []
            for group in self.groups[self.level]:
                md, ms = 0, 0
                for b, (axis, mask, _) in enumerate(group):
                    if m >> b & 1:
                        md, ms = (md | mask, ms) if axis == "dp" else (md, ms | mask)
                both.append((md, ms))
            out.append(both)
        return out

    def permute(self, value, both):
        nd, ns = self.dims
        pairs = []
        for d in range(nd):
            for q in range(ns):
                md, ms = both[q & 1]
                pairs.append((d * ns + q, (d ^ md) * ns + (q ^ ms)))
        return lax.ppermute(value, ("dp", "seq"), pairs)

    def index(self, level):
        idx = [jnp.int32(0), jnp.int32(0)]
        for i, group in enumerate(self.groups[level]):
            for b, st in enumerate(group):
                idx[i] = idx[i] + (st[2] << b)
        return jnp.where(self.parity == 0, idx[0], idx[1])

    def plan(self):
        if not self.back:
            last = self.level == len(self.groups) - 1
            parts = 1 if last else 1 << len(self.groups[self.level + 1][0])
            return ("sum", len(self.held), parts, self.lo, self.rows), (jnp.int32(0) if last else self.index(self.level + 1))
        return ("join", len(self.held), 1, 0, self.rows * len(self.held)), self.index(self.level)

    def landed(self, outs):
        (kind, held, parts, _, rows), _ = self.plan()
        self.lo = 0
        if kind == "sum":
            self.rows = rows // parts
            self.own, sends = outs[0], outs[1:]
            if parts == 1:
                self.back = True
                sends = [self.own] * (len(self.masks()))
            else:
                self.level += 1
        else:
            self.rows = rows
            self.own = outs[0]
            self.level -= 1
            if self.level < 0:
                self.done = True
                return
            sends = [self.own] * (len(self.masks()))
        self.sends = sends
        self.held = [self.own] + [self.permute(v, m) for v, m in zip(sends, self.masks())]


def advance(chains, name="advance"):
    chains = [c for c in chains if not c.done]
    if not chains:
        return []
    plans = [c.plan() for c in chains]
    D = chains[0].held[0].shape[1]
    ins, outs, tmp = [], [], []
    for c, (p, _) in zip(chains, plans):
        ins += c.held
        kind, held, parts, _, rows = p
        outs += [((rows // parts, D), bf16)] * parts if kind == "sum" else [((rows, D), bf16)]
        tmp.append(((rows, D) if kind == "sum" and parts > 1 else (16, D), bf16))
    idx = jnp.stack([i for _, i in plans]).astype(jnp.int32)
    got = call(functools.partial(advance_body, plan=[p for p, _ in plans], taken=len(ins)), (idx, *ins), outs, tmp[::-1],
               specs=[SMEM] + [VMEM] * len(ins), name=name)
    at, sends = 0, []
    for c, (p, _) in zip(chains, plans):
        n = p[2] if p[0] == "sum" else 1
        c.landed(got[at : at + n])
        at += n
        if not c.done:
            sends += c.sends
    return sends


def first_cut(chain):
    parts = 1 << len(chain.groups[0][0])
    size, idx = chain.rows // parts, chain.index(0)
    outs = []
    for m in range(parts):
        start = (idx ^ m) * size
        a, b = (lax.dynamic_slice_in_dim(v, start, size, 0) for v in chain.held)
        outs.append(a + b)
    chain.landed(outs)
    return chain.sends


def ordered(chains, *after):
    chains = [c for c in chains if not c.done]
    if not chains:
        return
    held = gate([c.held for c in chains], *after)
    for c, h in zip(chains, held):
        c.held = h


def core_swap(value, ns):
    return lax.ppermute(value, "seq", xor_pairs(ns, 1))


def gate(value, *deps):
    flat, tree = jax.tree.flatten(value)
    extra, _ = jax.tree.flatten(deps)
    outs = ob(tuple(flat) + tuple(extra))
    return jax.tree.unflatten(tree, outs[: len(flat)])


def exchange_in(arr, me, size):
    pieces = []
    for k in range(4):
        part = lax.dynamic_slice_in_dim(arr, 2 * (me ^ k), 2, 0)
        pieces.append(lax.ppermute(part, "seq", xor_pairs(size, k)) if k else part)
    return pieces


def exchange_out(pieces, size):
    return [lax.ppermute(p, "seq", xor_pairs(size, k)) if k else p for k, p in enumerate(pieces)]


def assemble_body(at_ref, p0, p1, p2, p3, out_ref):
    me = at_ref[0]
    for k, piece in enumerate((p0, p1, p2, p3)):
        out_ref[pl.ds(2 * (me ^ k), 2)] = piece[...]


def assemble(at, pieces):
    out = ((8,) + pieces[0].shape[1:], bf16)
    return call(assemble_body, (at, *pieces), [out], specs=[SMEM] + [VMEM] * 4, name="assemble")[0]


def final_ffn_body(at_ref, mine, other, w1_ref, w2_ref, wo_ref):
    core = at_ref[1]
    blocks = w1_ref.shape[1] // 512
    for src, c in ((mine, core), (other, 1 - core)):
        for j in range(blocks // 2):
            cs = pl.ds(pl.multiple_of((c * (blocks // 2) + j) * 512, 512), 512)
            w1_ref[:, cs] = src[2 * j * 512 : (2 * j + 1) * 512].astype(f32)
            w2_ref[cs, :] = src[(2 * j + 1) * 512 : (2 * j + 2) * 512].astype(f32)
        wo_ref[pl.ds(pl.multiple_of(c * 256, 256), 256), :] = src[blocks * 512 : blocks * 512 + 256].astype(f32)


def final_rest_body(at_ref, mine, other, c_ref, co_ref, s_ref, sb_ref, cb_ref, gg_ref, gb_ref, b1_ref, b2_ref, vec_ref):
    core = at_ref[1]
    for src, c in ((mine, core), (other, 1 - core)):
        cs = pl.ds(pl.multiple_of(c * 256, 256), 256)
        for j in range(3):
            c_ref[j, cs, :] = src[j * 256 : (j + 1) * 256].astype(f32)
            s_ref[j, cs, :] = src[1024 + j * 256 : 1024 + (j + 1) * 256].astype(f32)
        co_ref[cs, :] = src[768:1024].astype(f32)
        vec_ref[pl.ds(pl.multiple_of(c * 16, 16), 16), :] = src[1792:1808].astype(f32)
    for out, rows in ((sb_ref, (0, 1, 12)), (cb_ref, (8, 9, 21)), (gg_ref, (10, 19, 16)), (gb_ref, (11, 20, 17))):
        for i, row in enumerate(rows):
            out[i : i + 1] = vec_ref[row : row + 1]
    b2_ref[...] = vec_ref[18:19]
    b1_ref[...] = vec_ref[24 : 24 + b1_ref.shape[0]]


def local(sizes, target_in, memory, target_seg, memory_seg, self_qkv, self_bias, self_out, cross_qkv, cross_bias, cross_out, w1, b1, w2, b2, gain, nb, cotangent):
    T, D = 512, 512
    N = 2 * T
    FF = w1.shape[1]
    ns, nd = sizes["seq"], sizes["dp"]
    dims = (nd, ns)
    me = lax.axis_index("seq")
    dp = lax.axis_index("dp")
    at = jnp.stack([me, me & 1]).astype(jnp.int32)
    other = ("seq", 2, (me >> 1) & 1)
    ds = []
    m = 1
    while m < nd:
        ds.append(("dp", m, (dp // m) & 1))
        m *= 2
    core = me & 1

    def levels(even, odd, cuts=()):
        out, i = [], 0
        for n in list(cuts) + [1] * len(even):
            if i < len(even):
                out.append((even[i : i + n], odd[i : i + n]))
                i += n
        return out

    yzx, xyz = ds + [other], [other] + ds
    zyx = ds[1:2] + ds[0:1] + [other] + ds[2:]

    unit = 8 * ns * nd

    def padded(rows):
        return -(-rows // unit) * unit

    piece = [((2, 128, D), bf16)] * 4
    act2 = ((2, T, D), bf16)
    flat = ((N, D), bf16)
    saved = [((2, D, T), bf16), ((2, 4, 8, T), f32), ((N, D), f32), ((N, 128), f32)]

    xp = call(cut_body, (at, target_in, target_seg, memory_seg), [((2, 144, D), bf16)] * 4, specs=[SMEM] + [VMEM] * 3, name="cut", us=1)
    xp = exchange_out(xp, ns)
    memory = gate(memory, xp)
    mp = exchange_in(memory, me, ns)
    cotangent = gate(cotangent, mp)
    cp = exchange_in(cotangent, me, ns)
    xx, seg, qs, ks, vs, ot1, log1, n1, inv1 = call(
        self_fwd_body, (at, *xp, self_qkv, self_bias, self_out), [act2, ((2, 8, T), f32), act2, act2, act2] + saved,
        specs=[SMEM] + [VMEM] * 7, name="self_fwd", us=12)
    mm, yb, qc, kc, vc, ot2, log2, n2, inv2 = call(
        cross_fwd_body, (at, n1, seg, *mp, cross_qkv, cross_bias, cross_out, gain, nb), [flat, flat, act2, act2, act2] + saved,
        specs=[SMEM] + [VMEM] * 11, name="cross_fwd", us=14)
    h1, h2 = padded(FF + 256), 1024
    h3 = padded(1808) - h2
    *rp, g2, f2, keep, send, vec3, db1 = call(
        ffn_body, (at, n2, inv2, ot2, *cp, w1, b1.reshape(1, FF), w2, b2.reshape(1, D), gain, nb),
        piece + [((N, D), f32), flat, ((h1, D), bf16), ((h1, D), bf16), ((8, D), f32), ((FF // D, D), f32)],
        [flat, ((N, FF), f32), ((N, FF), bf16), ((N, FF), bf16), flat, flat, flat],
        specs=[SMEM] + [VMEM] * 13, name="ffn", us=23)
    got = core_swap(send, ns)

    def half_specs(p):
        cut = pl.BlockSpec((2, T, 256), lambda i: (0, 0, p))
        return [VMEM] + [cut] * 3 + [pl.BlockSpec((2, 256, T), lambda i: (0, p, 0)), pl.BlockSpec((2, 2, 8, T), lambda i: (0, p, 0, 0)), VMEM, pl.BlockSpec((256, D), lambda i: (p, 0))]

    half3 = [((N, 256), bf16)] * 3
    dca = call(functools.partial(bwd_first_body, causal=False), (f2, qc, kc, vc, ot2, log2, seg, cross_out), half3, specs=half_specs(0), grid=(1,), name="cross_bwd_a", us=10)
    dca, got = ob((dca, got))
    big = [Chain(dims, core, (keep, got), h1, levels(yzx, zyx))]
    s = first_cut(big[0])
    dca, rp = gate((dca, rp), s)
    rp = exchange_out(rp, ns)
    *gp, g1, f1, keep, send, vec2, dkc, dvc = call(
        cross_second_body, (at, f2, qc, kc, vc, ot2, log2, seg, cross_out, *dca, g2, n1, inv1, ot1, cross_qkv, gain, yb, mm),
        piece + [((N, D), f32), flat, ((h2, D), bf16), ((h2, D), bf16), ((8, D), f32), flat, flat], [flat] * 2,
        specs=[SMEM] + half_specs(1) + [VMEM] * 11, grid=(1,), name="cross_bwd_b", us=13)
    got = core_swap(send, ns)
    ordered(big, f1)
    s = advance(big)
    f1, rp = gate((f1, rp), s)
    f1, rp = ob((f1, rp))
    dsa = call(functools.partial(bwd_first_body, causal=True), (f1, qs, ks, vs, ot1, log1, seg, self_out), half3, specs=half_specs(0), grid=(1,), name="self_bwd_a", us=9)
    dsa, got = ob((dsa, got))
    ordered(big, dsa)
    s = advance(big)
    dsa, gp = gate((dsa, gp), s)
    gp = exchange_out(gp, ns)
    keep2, got2 = keep, got
    db1 = jnp.roll(db1, 2 * core, axis=0)
    dd = call(
        self_second_body, (f1, qs, ks, vs, ot1, log1, seg, self_out, *dsa), [((3, N, D), bf16)],
        specs=half_specs(1) + [VMEM] * 3, grid=(1,), name="self_bwd_b", us=7)[0]
    dd, gp = ob((dd, gp))
    ordered(big, dd)
    s = advance(big)
    keep, send = call(self_weights_body, (at, gate(dd, s), xx.reshape(N, D), vec2, vec3, db1), [((h3, D), bf16), ((h3, D), bf16)],
                      specs=[SMEM] + [VMEM] * 5, name="self_weights", us=4)
    got = core_swap(send, ns)
    rest = [Chain(dims, core, (keep2, got2, keep, got), h2 + h3, levels(yzx, xyz))]
    tp = call(target_grad_body, (at, gate(g1, send), self_qkv, dd), piece, [flat], specs=[SMEM] + [VMEM] * 3, name="target_grad", us=3)
    ordered(rest, tp)
    last = advance(rest)
    tp = exchange_out(gate(tp, last), ns)
    for what in ("big", "rest", "big", "rest", "halves", "big", "rest", "target", "big", "rest", "rest", "big", "rest", "ffn", "rest", "rest"):
        if what == "big" and not big[0].done:
            ordered(big, last)
            last = (last, advance(big))
            if big[0].done:
                other_half = core_swap(gate(big[0].own, last), ns)
        elif what == "rest" and not rest[0].done:
            ordered(rest, last)
            last = (last, advance(rest))
        elif what == "halves":
            result, mgrad = assemble(at, gate(rp, last)), assemble(at, gate(gp, last))
            last = (last, result, mgrad, tp[1], tp[2])
        elif what == "target":
            tgrad = assemble(at, gate(tp, last))
            last = (last, tgrad)
        elif what == "ffn":
            while not big[0].done:
                advance(big)
                other_half = core_swap(big[0].own, ns)
            gw = call(final_ffn_body, (at, big[0].own, gate(other_half, last)), [((D, FF), f32), ((FF, D), f32), ((D, D), f32)],
                      specs=[SMEM] + [VMEM] * 2, name="final_ffn", us=5)
            last = (last, gw)
    while not rest[0].done:
        advance(rest)
    gw1, gw2, gwo2 = gw
    gcw, gwo1, gsw, dsb, dcb, gg, gb, gb1, gb2 = call(
        final_rest_body, (at, rest[0].own, core_swap(rest[0].own, ns)),
        [((3, D, D), f32), ((D, D), f32), ((3, D, D), f32)] + [((3, D), f32)] * 4 + [((FF // D, D), f32), ((1, D), f32)], [((32, D), f32)],
        specs=[SMEM, VMEM, VMEM], name="final_rest", us=3)
    return result, tgrad, mgrad, gsw, dsb, gwo1, gcw, dcb, gwo2, gw1, gb1.reshape(FF), gw2, gb2.reshape(D), gg, gb


def solution(mesh):
    from jax.sharding import PartitionSpec as P

    act, seg, rep = P("dp", "seq", None), P("dp", "seq"), P()
    return jax.shard_map(
        functools.partial(local, dict(mesh.shape)),
        mesh=mesh,
        in_specs=(act, act, seg, seg) + (rep,) * 12 + (act,),
        out_specs=(act, act, act) + (rep,) * 12,
        check_vma=False,
    )
```

```python
import functools
import jax
import jax.numpy as jnp
from jax import lax
from jax.experimental import pallas as pl
from jax.experimental.pallas import tpu as pltpu

bf16 = jnp.bfloat16
f32 = jnp.float32
BIG = 1e9
EPS = 1e-5
HD = 64
FFN_TB = 512


def nn(a, b):
    return jnp.dot(a, b, preferred_element_type=f32)


def nt(a, b):
    return lax.dot_general(a, b, (((1,), (1,)), ((), ())), preferred_element_type=f32)


def tn(a, b):
    return lax.dot_general(a, b, (((0,), (0,)), ((), ())), preferred_element_type=f32)


def ln_fwd(h):
    c = h - jnp.mean(h, axis=-1, keepdims=True)
    inv = lax.rsqrt(jnp.mean(c * c, axis=-1, keepdims=True) + EPS)
    return c * inv, inv


def ln_bwd(up, n, inv, gain):
    e = up * gain
    return inv * (e - jnp.mean(e, axis=-1, keepdims=True) - n * jnp.mean(e * n, axis=-1, keepdims=True))


def colsum(v):
    return jnp.sum(v.astype(f32), axis=0, keepdims=True)


def key_marks(seg_row):
    count = seg_row.shape[1]
    seg = jnp.transpose(jnp.broadcast_to(seg_row, (128, count)))
    lane = lax.broadcasted_iota(jnp.int32, (count, 128), 1)
    off = (lane.astype(f32) != seg) & (lane < 16)
    return jnp.where(off | ((lane >= 16) & (lane < 19)), 1.0, 0.0).astype(bf16)


def query_marks(seg_row):
    count = seg_row.shape[1]
    sub = lax.broadcasted_iota(jnp.int32, (16, count), 0)
    return jnp.where(sub.astype(f32) == seg_row, -BIG, 0.0).astype(bf16)


def split_rows(row):
    hi = row.astype(bf16)
    rest = row - hi.astype(f32)
    mid = rest.astype(bf16)
    low = (rest - mid.astype(f32)).astype(bf16)
    sub = lax.broadcasted_iota(jnp.int32, (16, row.shape[1]), 0)
    out = jnp.where(sub == 0, hi.astype(f32), jnp.where(sub == 1, mid.astype(f32), jnp.where(sub == 2, low.astype(f32), 0.0)))
    return out.astype(bf16)


def causal_keep(keys, queries):
    k = lax.broadcasted_iota(jnp.int32, (keys, queries), 0)
    q = lax.broadcasted_iota(jnp.int32, (keys, queries), 1)
    return k <= q


def head_rows(pair_t, which):
    z = jnp.zeros((HD, pair_t.shape[1]), bf16)
    part = pair_t[which * HD : (which + 1) * HD]
    return [part, z] if which == 0 else [z, part]


def key_blocks(count_q, count_k, causal):
    if not causal:
        return [(0, count_k, 0)]
    half = count_k // 2
    return [(0, half, 0), (half, count_k, half)]


def masked_scores(lhs, rhs, block, causal):
    lo, hi, first = block
    s = nn(lhs[lo:hi], rhs[:, first:])
    if causal:
        size = hi - lo
        diag = jnp.where(causal_keep(size, size), s[:, :size], -BIG)
        s = diag if s.shape[1] == size else jnp.concatenate([diag, s[:, size:]], axis=1)
    return s


def attend_pair_fwd(q_pair, k_pair, v_pair, kmarks, qmarks, causal):
    count_q, count_k = q_pair.shape[0], k_pair.shape[0]
    qt = jnp.transpose(q_pair)
    vt = jnp.transpose(v_pair)
    lhs = jnp.concatenate([k_pair, kmarks], axis=1)
    pad = jnp.zeros((112, count_q), bf16)
    ones = jnp.ones((16, count_k), bf16)
    outs, logs = [], []
    for h in range(2):
        rhs = jnp.concatenate(head_rows(qt, h) + [qmarks, pad], axis=0)
        vh = jnp.concatenate([vt[h * HD : (h + 1) * HD], ones], axis=0)
        if causal:
            half = count_k // 2
            s0, s1 = (masked_scores(lhs, rhs, b, True) for b in key_blocks(count_q, count_k, True))
            top = jnp.max(s0, axis=0, keepdims=True)
            late = jnp.maximum(top[:, half:], jnp.max(s1, axis=0, keepdims=True))
            top = jnp.concatenate([top[:, :half], late], axis=1)
            o0 = nn(vh[:, :half], jnp.exp(s0 - top).astype(bf16))
            o1 = nn(vh[:, half:], jnp.exp(s1 - late).astype(bf16))
            o = jnp.concatenate([o0[:, :half], o0[:, half:] + o1], axis=1)
        else:
            s = nn(lhs, rhs)
            top = jnp.max(s, axis=0, keepdims=True)
            o = nn(vh, jnp.exp(s - top).astype(bf16))
        total = o[HD : HD + 1]
        outs.append((o[:HD] * (1.0 / total)).astype(bf16))
        logs.append(top + jnp.log(total))
    return jnp.concatenate(outs, axis=0), logs


def attend_pair_bwd(q_pair, k_pair, v_pair, do_pair, ot_pair, logs, kmarks, qmarks, causal):
    count_q, count_k = q_pair.shape[0], k_pair.shape[0]
    qt = jnp.transpose(q_pair)
    kt = jnp.transpose(k_pair)
    dot_ = jnp.transpose(do_pair)
    inner = dot_.astype(f32) * ot_pair.astype(f32)
    lhs_s = jnp.concatenate([k_pair, kmarks], axis=1)
    lhs_p = jnp.concatenate([v_pair, kmarks], axis=1)
    pad = jnp.zeros((96, count_q), bf16)
    z16 = jnp.zeros((16, count_q), bf16)
    lane_q = lax.broadcasted_iota(jnp.int32, (count_q, 128), 1)
    zero = jnp.zeros((count_q, 128), bf16)
    blocks = key_blocks(count_q, count_k, causal)
    dq_t, dk, dv = [], [None] * len(blocks), [None] * len(blocks)
    for h in range(2):
        rhs_s = jnp.concatenate(head_rows(qt, h) + [qmarks, split_rows(-logs[h]), pad], axis=0)
        d = jnp.sum(inner[h * HD : (h + 1) * HD], axis=0, keepdims=True)
        rhs_p = jnp.concatenate(head_rows(dot_, h) + [z16, split_rows(-d), pad], axis=0)
        mine = (lane_q < HD) if h == 0 else (lane_q >= HD)
        do_h, q_h = jnp.where(mine, do_pair, zero), jnp.where(mine, q_pair, zero)
        dq = None
        for i, (lo, hi, first) in enumerate(blocks):
            p = jnp.exp(masked_scores(lhs_s, rhs_s, (lo, hi, first), causal))
            g = nn(lhs_p[lo:hi], rhs_p[:, first:])
            ds = (p * g).astype(bf16)
            v_part = nn(p.astype(bf16), do_h[first:])
            k_part = nn(ds, q_h[first:])
            q_part = nn(kt[h * HD : (h + 1) * HD, lo:hi], ds)
            dq = q_part if dq is None else jnp.concatenate([dq[:, :first], dq[:, first:] + q_part], axis=1)
            dv[i] = v_part if dv[i] is None else dv[i] + v_part
            dk[i] = k_part if dk[i] is None else dk[i] + k_part
        dq_t.append(dq * 0.125)
    dq = jnp.transpose(jnp.concatenate(dq_t, axis=0).astype(bf16))
    join = lambda parts: parts[0] if len(parts) == 1 else jnp.concatenate(parts, axis=0)
    return dq, join(dk).astype(bf16), join(dv).astype(bf16)


VMEM = pl.BlockSpec(memory_space=pltpu.VMEM)
SMEM = pl.BlockSpec(memory_space=pltpu.SMEM)
ob = lax.optimization_barrier


def call(body, ins, outs, scratch=(), specs=None, grid=(), limit=50 << 20, us=1, name=None):
    return pl.pallas_call(
        body,
        grid=grid,
        in_specs=specs or [VMEM] * len(ins),
        out_specs=[VMEM] * len(outs),
        out_shape=[jax.ShapeDtypeStruct(s, d) for s, d in outs],
        scratch_shapes=[pltpu.VMEM(s, d) for s, d in scratch],
        compiler_params=pltpu.CompilerParams(vmem_limit_bytes=limit),
        cost_estimate=pl.CostEstimate(flops=us * 1_000_000_000, bytes_accessed=1 << 20, transcendentals=0),
        name=name,
    )(*ins)


def piece_start(me, k):
    return pl.multiple_of((me ^ k) * 128, 128)


def fwd_attention(q_ref, k_ref, v_ref, ot_ref, log_ref, kmarks, qmarks, causal):
    for p in range(4):
        c = slice(p * 128, (p + 1) * 128)
        ot, logs = attend_pair_fwd(q_ref[:, c], k_ref[:, c], v_ref[:, c], kmarks, qmarks, causal)
        ot_ref[c, :] = ot
        for h in range(2):
            log_ref[p, h : h + 1, :] = logs[h]


def cut_body(at_ref, x_ref, ts_ref, ms_ref, o0, o1, o2, o3):
    me = at_ref[0]
    segs = [r[...].astype(f32) for r in (ts_ref, ms_ref)]
    sub = lax.broadcasted_iota(jnp.int32, segs[0].shape, 0)
    for k, out in enumerate((o0, o1, o2, o3)):
        for r in range(2):
            row = 2 * (me ^ k) + r
            out[r, 0:128] = x_ref[row]
            line = [jnp.sum(jnp.where(sub == row, sg, 0.0), axis=0, keepdims=True) for sg in segs]
            line = jnp.concatenate(line + [jnp.zeros((1, 256), f32)], axis=1)
            out[r, 128:144] = jnp.broadcast_to(line, (16, 512)).astype(bf16)


def self_fwd_body(at_ref, x0, x1, x2, x3, w_ref, b_ref, wo_ref, x_ref, seg_ref, q_ref, k_ref, v_ref, ot_ref, log_ref, n_ref, inv_ref):
    me = at_ref[0]
    for r in range(2):
        for k, piece in enumerate((x0, x1, x2, x3)):
            at = piece_start(me, k)
            x_ref[r, pl.ds(at, 128), :] = piece[r, 0:128]
            marks = piece[r, 128:144].astype(f32)
            seg_ref[r, 0:1, pl.ds(at, 128)] = marks[0:1, 0:128]
            seg_ref[r, 1:2, pl.ds(at, 128)] = marks[0:1, 128:256]
    for r in range(2):
        x = x_ref[r]
        q_ref[r] = (nn(x, w_ref[0]) + b_ref[0:1]).astype(bf16) * jnp.asarray(0.125, bf16)
        k_ref[r] = nn(x, w_ref[1]).astype(bf16)
        v_ref[r] = (nn(x, w_ref[2]) + b_ref[1:2]).astype(bf16)
        seg = seg_ref[r, 0:1]
        fwd_attention(q_ref.at[r], k_ref.at[r], v_ref.at[r], ot_ref.at[r], log_ref.at[r], key_marks(seg), query_marks(seg), True)
        h = x_ref[r].astype(f32) + tn(ot_ref[r], wo_ref[...]) + b_ref[2:3]
        n, inv = ln_fwd(h)
        rows = slice(r * 512, (r + 1) * 512)
        n_ref[rows] = n
        inv_ref[rows] = jnp.broadcast_to(inv, (h.shape[0], 128))


def cross_fwd_body(at_ref, n1_ref, seg_ref, m0, m1, m2, m3, w_ref, b_ref, wo_ref, gain_ref, off_ref, m_ref, y_ref, q_ref, k_ref, v_ref, ot_ref, log_ref, n_ref, inv_ref):
    me = at_ref[0]
    for r in range(2):
        rows = slice(r * 512, (r + 1) * 512)
        for k, piece in enumerate((m0, m1, m2, m3)):
            m_ref[pl.ds(r * 512 + piece_start(me, k), 128), :] = piece[r]
        y_ref[rows] = (n1_ref[rows] * gain_ref[0:1] + off_ref[0:1]).astype(bf16)
        m = m_ref[rows]
        q_ref[r] = (nn(y_ref[rows], w_ref[0]) + b_ref[0:1]).astype(bf16) * jnp.asarray(0.125, bf16)
        k_ref[r] = nn(m, w_ref[1]).astype(bf16)
        v_ref[r] = (nn(m, w_ref[2]) + b_ref[1:2]).astype(bf16)
        fwd_attention(q_ref.at[r], k_ref.at[r], v_ref.at[r], ot_ref.at[r], log_ref.at[r], key_marks(seg_ref[r, 1:2]), query_marks(seg_ref[r, 0:1]), False)
        h = n1_ref[rows] * gain_ref[0:1] + off_ref[0:1] + tn(ot_ref[r], wo_ref[...]) + b_ref[2:3]
        n, inv = ln_fwd(h)
        n_ref[rows] = n
        inv_ref[rows] = jnp.broadcast_to(inv, (h.shape[0], 128))


def spread(at_ref, value_ref, pieces):
    me = at_ref[0]
    for k in range(4):
        for r in range(2):
            pieces[k][r] = value_ref[pl.ds(r * 512 + piece_start(me, k), 128), :]


def fill_rest(ref, start):
    if ref.shape[0] > start:
        ref[start:] = jnp.zeros((ref.shape[0] - start, ref.shape[1]), ref.dtype)


def ffn_body(at_ref, n_in_ref, inv_in_ref, ot_ref, c0, c1, c2, c3, w1_ref, b1_ref, w2_ref, b2_ref, gain_ref, nb_ref,
             r0, r1, r2, r3, g_ref, f2_ref, keep_ref, send_ref, vec_ref, db1_ref, yb_ref, u_ref, a_ref, du_ref, f_ref, ct_ref, res_ref):
    me, core = at_ref[0], at_ref[1]
    for k, piece in enumerate((c0, c1, c2, c3)):
        for r in range(2):
            ct_ref[pl.ds(r * 512 + piece_start(me, k), 128), :] = piece[r]
    core = at_ref[1]
    FC, TB = 512, FFN_TB
    blocks = w1_ref.shape[1] // FC
    sums = [0.0] * 6
    for t in range(n_in_ref.shape[0] // TB):
        ts = slice(t * TB, (t + 1) * TB)
        y = n_in_ref[ts] * gain_ref[1:2] + nb_ref[1:2]
        yb = y.astype(bf16)
        yb_ref[ts] = yb
        for c in range(blocks):
            cs = slice(c * FC, (c + 1) * FC)
            u = nn(yb, w1_ref[:, cs]) + b1_ref[:, cs]
            sg = 0.5 * jnp.tanh(0.5 * u) + 0.5
            u_ref[ts, cs] = (sg * (1.0 + u * (1.0 - sg)))
            a_ref[ts, cs] = (u * sg).astype(bf16)
        n, inv = ln_fwd(y + nn(a_ref[ts], w2_ref[...]) + b2_ref[...])
        res_ref[ts] = (n * gain_ref[2:3] + nb_ref[2:3]).astype(bf16)
        up = ct_ref[ts].astype(f32)
        g3 = ln_bwd(up, n, inv, gain_ref[2:3])
        f3 = g3.astype(bf16)
        f_ref[ts] = f3
        sums[0], sums[1], sums[2] = sums[0] + colsum(up * n), sums[1] + colsum(up), sums[2] + colsum(f3)
        for c in range(blocks):
            cs = slice(c * FC, (c + 1) * FC)
            du_ref[ts, cs] = (nt(f3, w2_ref[cs, :]) * u_ref[ts, cs]).astype(bf16)
        up = g3 + nt(du_ref[ts], w1_ref[...])
        n = n_in_ref[ts]
        g2 = ln_bwd(up, n, inv_in_ref[ts, 0:1], gain_ref[1:2])
        g_ref[ts] = g2
        f2 = g2.astype(bf16)
        f2_ref[ts] = f2
        sums[3], sums[4], sums[5] = sums[3] + colsum(up * n), sums[4] + colsum(up), sums[5] + colsum(f2)
    for i in range(6):
        vec_ref[i : i + 1] = sums[i]
    vec_ref[6:8] = jnp.zeros((2, vec_ref.shape[1]), f32)
    spread(at_ref, res_ref, (r0, r1, r2, r3))
    for c in range(blocks):
        block = (core * (blocks // 2) + c) % blocks
        cs = pl.ds(pl.multiple_of(block * FC, FC), FC)
        out = keep_ref if c < blocks // 2 else send_ref
        base = 2 * (c % (blocks // 2)) * FC
        out[base + FC : base + 2 * FC] = tn(a_ref[:, cs], f_ref[...]).astype(bf16)
        db1_ref[c : c + 1] = colsum(du_ref[:, cs])
        out[base : base + FC] = tn(yb_ref[...], du_ref[:, cs]).astype(bf16)
    base = blocks * FC
    for out, c in ((keep_ref, core), (send_ref, 1 - core)):
        cs = pl.ds(pl.multiple_of(c * 256, 256), 256)
        out[base : base + 256] = (nn(ot_ref[0, cs, :], f2_ref[0:512]) + nn(ot_ref[1, cs, :], f2_ref[512:1024])).astype(bf16)
        fill_rest(out, base + 256)


def attention_bwd(causal, f_ref, q_ref, k_ref, v_ref, o_ref, l_ref, seg_ref, wo_ref, dq_ref, dk_ref, dv_ref):
    for r in range(2):
        rows = slice(r * 512, (r + 1) * 512)
        do = nt(f_ref[rows], wo_ref[...]).astype(bf16)
        km = key_marks(seg_ref[r, 0:1] if causal else seg_ref[r, 1:2])
        qm = query_marks(seg_ref[r, 0:1])
        for p in range(q_ref.shape[2] // 128):
            c = slice(p * 128, (p + 1) * 128)
            logs = [l_ref[r, p, h : h + 1, :] for h in range(2)]
            dq, dk, dv = attend_pair_bwd(q_ref[r, :, c], k_ref[r, :, c], v_ref[r, :, c], do[:, c], o_ref[r, c, :], logs, km, qm, causal)
            dq_ref[rows, c] = dq
            dk_ref[rows, c] = dk
            dv_ref[rows, c] = dv


def bwd_first_body(f_ref, q_ref, k_ref, v_ref, o_ref, l_ref, seg_ref, wo_ref, dq_ref, dk_ref, dv_ref, causal):
    attention_bwd(causal, f_ref, q_ref, k_ref, v_ref, o_ref, l_ref, seg_ref, wo_ref, dq_ref, dk_ref, dv_ref)


def cross_second_body(at_ref, f_ref, q_ref, k_ref, v_ref, o_ref, l_ref, seg_ref, wo_ref, dqa, dka, dva, g_ref, n1_ref, inv1_ref, ot1_ref, w_ref, gain_ref, y_ref, m_ref,
                      p0, p1, p2, p3, g1_ref, f1_ref, keep_ref, send_ref, vec_ref, dk_ref, dv_ref, dq_ref, mg_ref):
    core = at_ref[1]
    attention_bwd(False, f_ref, q_ref, k_ref, v_ref, o_ref, l_ref, seg_ref, wo_ref, dq_ref.at[:, 256:512], dk_ref.at[:, 256:512], dv_ref.at[:, 256:512])
    for old, new in ((dqa, dq_ref), (dka, dk_ref), (dva, dv_ref)):
        new[:, 0:256] = old[...]
    mg_ref[...] = (nt(dk_ref[...], w_ref[1]) + nt(dv_ref[...], w_ref[2])).astype(bf16)
    spread(at_ref, mg_ref, (p0, p1, p2, p3))
    vec_ref[0:1] = colsum(dq_ref[...])
    vec_ref[1:2] = colsum(dv_ref[...])
    up = g_ref[...] + nt(dq_ref[...], w_ref[0])
    n = n1_ref[...]
    g1 = ln_bwd(up, n, inv1_ref[:, 0:1], gain_ref[0:1])
    g1_ref[...] = g1
    f1 = g1.astype(bf16)
    f1_ref[...] = f1
    vec_ref[2:3] = colsum(up * n)
    vec_ref[3:4] = colsum(up)
    vec_ref[4:5] = colsum(f1)
    vec_ref[5:8] = jnp.zeros((3, vec_ref.shape[1]), f32)
    for out, c in ((keep_ref, core), (send_ref, 1 - core)):
        cs = pl.ds(pl.multiple_of(c * 256, 256), 256)
        out[0:256] = tn(y_ref[:, cs], dq_ref[...]).astype(bf16)
        out[256:512] = tn(m_ref[:, cs], dk_ref[...]).astype(bf16)
        out[512:768] = tn(m_ref[:, cs], dv_ref[...]).astype(bf16)
        out[768:1024] = (nn(ot1_ref[0, cs, :], f1_ref[0:512]) + nn(ot1_ref[1, cs, :], f1_ref[512:1024])).astype(bf16)
        fill_rest(out, 1024)


def self_second_body(f_ref, q_ref, k_ref, v_ref, o_ref, l_ref, seg_ref, wo_ref, dqa, dka, dva, d_ref):
    attention_bwd(True, f_ref, q_ref, k_ref, v_ref, o_ref, l_ref, seg_ref, wo_ref, d_ref.at[0, :, 256:512], d_ref.at[1, :, 256:512], d_ref.at[2, :, 256:512])
    for j, old in enumerate((dqa, dka, dva)):
        d_ref[j, :, 0:256] = old[...]


def self_weights_body(at_ref, d_ref, x_ref, vec2_ref, vec3_ref, db1_ref, keep_ref, send_ref):
    core = at_ref[1]
    D = x_ref.shape[1]
    zero = jnp.zeros((1, D), f32)
    low = jnp.concatenate([colsum(d_ref[0]), colsum(d_ref[2])] + [zero] * 6 + [vec2_ref[...]], axis=0)
    high = jnp.concatenate([vec3_ref[...], db1_ref[...]] + [zero] * (8 - db1_ref.shape[0]), axis=0)
    pick = core == 0
    for out, c, swap in ((send_ref, 1 - core, True), (keep_ref, core, False)):
        cs = pl.ds(pl.multiple_of(c * 256, 256), 256)
        for j in range(3):
            out[j * 256 : (j + 1) * 256] = tn(x_ref[:, cs], d_ref[j]).astype(bf16)
        first, second = (high, low) if swap else (low, high)
        out[768:784] = jnp.where(pick, first, second).astype(bf16)
        fill_rest(out, 784)


def target_grad_body(at_ref, g_ref, w_ref, d_ref, p0, p1, p2, p3, tg_ref):
    tg_ref[...] = (g_ref[...] + nt(d_ref[0], w_ref[0]) + nt(d_ref[1], w_ref[1]) + nt(d_ref[2], w_ref[2])).astype(bf16)
    spread(at_ref, tg_ref, (p0, p1, p2, p3))


def xor_pairs(size, mask):
    return [(i, i ^ mask) for i in range(size)]


def advance_body(idx_ref, *refs, plan, taken):
    ins, outs = refs[:taken], refs[taken:]
    at_in, at_out = 0, 0
    for i, (kind, held, parts, lo, rows) in enumerate(plan):
        mine = ins[at_in : at_in + held]
        if kind == "sum":
            if lo:
                total = jnp.concatenate(
                    [mine[0][...].astype(f32) + mine[1][...].astype(f32), mine[2][...].astype(f32) + mine[3][...].astype(f32)], axis=0)
            else:
                total = mine[0][...].astype(f32)
                for ref in mine[1:]:
                    total = total + ref[...].astype(f32)
            if parts == 1:
                outs[at_out][...] = total.astype(bf16)
                at_out += 1
            else:
                tmp = outs[-1 - i]
                tmp[...] = total.astype(bf16)
                size = rows // parts
                for m in range(parts):
                    start = pl.multiple_of((idx_ref[i] ^ m) * size, 16)
                    outs[at_out + m][...] = tmp[pl.ds(start, size), :]
                at_out += parts
        else:
            size = rows // held
            for m in range(held):
                start = pl.multiple_of((idx_ref[i] ^ m) * size, 16)
                outs[at_out][pl.ds(start, size), :] = mine[m][...]
            at_out += 1
        at_in += held


class Chain:
    def __init__(self, dims, parity, held, rows, levels):
        self.dims, self.parity, self.held, self.lo, self.rows, self.groups = dims, parity, list(held), int(len(held) == 4), rows, levels
        self.level, self.back, self.done = -1, False, False

    def masks(self):
        out = []
        for m in range(1, 1 << len(self.groups[self.level][0])):
            both = []
            for group in self.groups[self.level]:
                md, ms = 0, 0
                for b, (axis, mask, _) in enumerate(group):
                    if m >> b & 1:
                        md, ms = (md | mask, ms) if axis == "dp" else (md, ms | mask)
                both.append((md, ms))
            out.append(both)
        return out

    def permute(self, value, both):
        nd, ns = self.dims
        pairs = []
        for d in range(nd):
            for q in range(ns):
                md, ms = both[q & 1]
                pairs.append((d * ns + q, (d ^ md) * ns + (q ^ ms)))
        return lax.ppermute(value, ("dp", "seq"), pairs)

    def index(self, level):
        idx = [jnp.int32(0), jnp.int32(0)]
        for i, group in enumerate(self.groups[level]):
            for b, st in enumerate(group):
                idx[i] = idx[i] + (st[2] << b)
        return jnp.where(self.parity == 0, idx[0], idx[1])

    def plan(self):
        if not self.back:
            last = self.level == len(self.groups) - 1
            parts = 1 if last else 1 << len(self.groups[self.level + 1][0])
            return ("sum", len(self.held), parts, self.lo, self.rows), (jnp.int32(0) if last else self.index(self.level + 1))
        return ("join", len(self.held), 1, 0, self.rows * len(self.held)), self.index(self.level)

    def landed(self, outs):
        (kind, held, parts, _, rows), _ = self.plan()
        self.lo = 0
        if kind == "sum":
            self.rows = rows // parts
            self.own, sends = outs[0], outs[1:]
            if parts == 1:
                self.back = True
                sends = [self.own] * (len(self.masks()))
            else:
                self.level += 1
        else:
            self.rows = rows
            self.own = outs[0]
            self.level -= 1
            if self.level < 0:
                self.done = True
                return
            sends = [self.own] * (len(self.masks()))
        self.sends = sends
        self.held = [self.own] + [self.permute(v, m) for v, m in zip(sends, self.masks())]


def advance(chains, name="advance"):
    chains = [c for c in chains if not c.done]
    if not chains:
        return []
    plans = [c.plan() for c in chains]
    D = chains[0].held[0].shape[1]
    ins, outs, tmp = [], [], []
    for c, (p, _) in zip(chains, plans):
        ins += c.held
        kind, held, parts, _, rows = p
        outs += [((rows // parts, D), bf16)] * parts if kind == "sum" else [((rows, D), bf16)]
        tmp.append(((rows, D) if kind == "sum" and parts > 1 else (16, D), bf16))
    idx = jnp.stack([i for _, i in plans]).astype(jnp.int32)
    got = call(functools.partial(advance_body, plan=[p for p, _ in plans], taken=len(ins)), (idx, *ins), outs, tmp[::-1],
               specs=[SMEM] + [VMEM] * len(ins), name=name)
    at, sends = 0, []
    for c, (p, _) in zip(chains, plans):
        n = p[2] if p[0] == "sum" else 1
        c.landed(got[at : at + n])
        at += n
        if not c.done:
            sends += c.sends
    return sends


def first_cut(chain):
    parts = 1 << len(chain.groups[0][0])
    size, idx = chain.rows // parts, chain.index(0)
    outs = []
    for m in range(parts):
        start = (idx ^ m) * size
        a, b = (lax.dynamic_slice_in_dim(v, start, size, 0) for v in chain.held)
        outs.append(a + b)
    chain.landed(outs)
    return chain.sends


def ordered(chains, *after):
    chains = [c for c in chains if not c.done]
    if not chains:
        return
    held = gate([c.held for c in chains], *after)
    for c, h in zip(chains, held):
        c.held = h


def core_swap(value, ns):
    return lax.ppermute(value, "seq", xor_pairs(ns, 1))


def gate(value, *deps):
    flat, tree = jax.tree.flatten(value)
    extra, _ = jax.tree.flatten(deps)
    outs = ob(tuple(flat) + tuple(extra))
    return jax.tree.unflatten(tree, outs[: len(flat)])


def exchange_in(arr, me, size):
    pieces = []
    for k in range(4):
        part = lax.dynamic_slice_in_dim(arr, 2 * (me ^ k), 2, 0)
        pieces.append(lax.ppermute(part, "seq", xor_pairs(size, k)) if k else part)
    return pieces


def exchange_out(pieces, size):
    return [lax.ppermute(p, "seq", xor_pairs(size, k)) if k else p for k, p in enumerate(pieces)]


def assemble_body(at_ref, p0, p1, p2, p3, out_ref):
    me = at_ref[0]
    for k, piece in enumerate((p0, p1, p2, p3)):
        out_ref[pl.ds(2 * (me ^ k), 2)] = piece[...]


def assemble(at, pieces):
    out = ((8,) + pieces[0].shape[1:], bf16)
    return call(assemble_body, (at, *pieces), [out], specs=[SMEM] + [VMEM] * 4, name="assemble")[0]


def final_ffn_body(at_ref, mine, other, w1_ref, w2_ref, wo_ref):
    core = at_ref[1]
    blocks = w1_ref.shape[1] // 512
    for src, c in ((mine, core), (other, 1 - core)):
        for j in range(blocks // 2):
            cs = pl.ds(pl.multiple_of((c * (blocks // 2) + j) * 512, 512), 512)
            w1_ref[:, cs] = src[2 * j * 512 : (2 * j + 1) * 512].astype(f32)
            w2_ref[cs, :] = src[(2 * j + 1) * 512 : (2 * j + 2) * 512].astype(f32)
        wo_ref[pl.ds(pl.multiple_of(c * 256, 256), 256), :] = src[blocks * 512 : blocks * 512 + 256].astype(f32)


def final_rest_body(at_ref, mine, other, c_ref, co_ref, s_ref, sb_ref, cb_ref, gg_ref, gb_ref, b1_ref, b2_ref, vec_ref):
    core = at_ref[1]
    for src, c in ((mine, core), (other, 1 - core)):
        cs = pl.ds(pl.multiple_of(c * 256, 256), 256)
        for j in range(3):
            c_ref[j, cs, :] = src[j * 256 : (j + 1) * 256].astype(f32)
            s_ref[j, cs, :] = src[1024 + j * 256 : 1024 + (j + 1) * 256].astype(f32)
        co_ref[cs, :] = src[768:1024].astype(f32)
        vec_ref[pl.ds(pl.multiple_of(c * 16, 16), 16), :] = src[1792:1808].astype(f32)
    for out, rows in ((sb_ref, (0, 1, 12)), (cb_ref, (8, 9, 21)), (gg_ref, (10, 19, 16)), (gb_ref, (11, 20, 17))):
        for i, row in enumerate(rows):
            out[i : i + 1] = vec_ref[row : row + 1]
    b2_ref[...] = vec_ref[18:19]
    b1_ref[...] = vec_ref[24 : 24 + b1_ref.shape[0]]


def local(sizes, target_in, memory, target_seg, memory_seg, self_qkv, self_bias, self_out, cross_qkv, cross_bias, cross_out, w1, b1, w2, b2, gain, nb, cotangent):
    T, D = 512, 512
    N = 2 * T
    FF = w1.shape[1]
    ns, nd = sizes["seq"], sizes["dp"]
    dims = (nd, ns)
    me = lax.axis_index("seq")
    dp = lax.axis_index("dp")
    at = jnp.stack([me, me & 1]).astype(jnp.int32)
    other = ("seq", 2, (me >> 1) & 1)
    ds = []
    m = 1
    while m < nd:
        ds.append(("dp", m, (dp // m) & 1))
        m *= 2
    core = me & 1

    def levels(even, odd, cuts=()):
        out, i = [], 0
        for n in list(cuts) + [1] * len(even):
            if i < len(even):
                out.append((even[i : i + n], odd[i : i + n]))
                i += n
        return out

    yzx, xyz = ds + [other], [other] + ds
    zyx = ds[1:2] + ds[0:1] + [other] + ds[2:]

    unit = 8 * ns * nd

    def padded(rows):
        return -(-rows // unit) * unit

    piece = [((2, 128, D), bf16)] * 4
    act2 = ((2, T, D), bf16)
    flat = ((N, D), bf16)
    saved = [((2, D, T), bf16), ((2, 4, 8, T), f32), ((N, D), f32), ((N, 128), f32)]

    xp = call(cut_body, (at, target_in, target_seg, memory_seg), [((2, 144, D), bf16)] * 4, specs=[SMEM] + [VMEM] * 3, name="cut", us=1)
    xp = exchange_out(xp, ns)
    memory = gate(memory, xp)
    mp = exchange_in(memory, me, ns)
    cotangent = gate(cotangent, mp)
    cp = exchange_in(cotangent, me, ns)
    xx, seg, qs, ks, vs, ot1, log1, n1, inv1 = call(
        self_fwd_body, (at, *xp, self_qkv, self_bias, self_out), [act2, ((2, 8, T), f32), act2, act2, act2] + saved,
        specs=[SMEM] + [VMEM] * 7, name="self_fwd", us=12)
    mm, yb, qc, kc, vc, ot2, log2, n2, inv2 = call(
        cross_fwd_body, (at, n1, seg, *mp, cross_qkv, cross_bias, cross_out, gain, nb), [flat, flat, act2, act2, act2] + saved,
        specs=[SMEM] + [VMEM] * 11, name="cross_fwd", us=14)
    h1, h2 = padded(FF + 256), 1024
    h3 = padded(1808) - h2
    *rp, g2, f2, keep, send, vec3, db1 = call(
        ffn_body, (at, n2, inv2, ot2, *cp, w1, b1.reshape(1, FF), w2, b2.reshape(1, D), gain, nb),
        piece + [((N, D), f32), flat, ((h1, D), bf16), ((h1, D), bf16), ((8, D), f32), ((FF // D, D), f32)],
        [flat, ((N, FF), f32), ((N, FF), bf16), ((N, FF), bf16), flat, flat, flat],
        specs=[SMEM] + [VMEM] * 13, name="ffn", us=23)
    got = core_swap(send, ns)

    def half_specs(p):
        cut = pl.BlockSpec((2, T, 256), lambda i: (0, 0, p))
        return [VMEM] + [cut] * 3 + [pl.BlockSpec((2, 256, T), lambda i: (0, p, 0)), pl.BlockSpec((2, 2, 8, T), lambda i: (0, p, 0, 0)), VMEM, pl.BlockSpec((256, D), lambda i: (p, 0))]

    half3 = [((N, 256), bf16)] * 3
    dca = call(functools.partial(bwd_first_body, causal=False), (f2, qc, kc, vc, ot2, log2, seg, cross_out), half3, specs=half_specs(0), grid=(1,), name="cross_bwd_a", us=10)
    dca, got = ob((dca, got))
    big = [Chain(dims, core, (keep, got), h1, levels(yzx, zyx))]
    s = first_cut(big[0])
    dca, rp = gate((dca, rp), s)
    rp = exchange_out(rp, ns)
    *gp, g1, f1, keep, send, vec2, dkc, dvc = call(
        cross_second_body, (at, f2, qc, kc, vc, ot2, log2, seg, cross_out, *dca, g2, n1, inv1, ot1, cross_qkv, gain, yb, mm),
        piece + [((N, D), f32), flat, ((h2, D), bf16), ((h2, D), bf16), ((8, D), f32), flat, flat], [flat] * 2,
        specs=[SMEM] + half_specs(1) + [VMEM] * 11, grid=(1,), name="cross_bwd_b", us=13)
    got = core_swap(send, ns)
    ordered(big, f1)
    s = advance(big)
    f1, rp = gate((f1, rp), s)
    f1, rp = ob((f1, rp))
    dsa = call(functools.partial(bwd_first_body, causal=True), (f1, qs, ks, vs, ot1, log1, seg, self_out), half3, specs=half_specs(0), grid=(1,), name="self_bwd_a", us=9)
    dsa, got = ob((dsa, got))
    ordered(big, dsa)
    s = advance(big)
    dsa, gp = gate((dsa, gp), s)
    gp = exchange_out(gp, ns)
    keep2, got2 = keep, got
    db1 = jnp.roll(db1, 2 * core, axis=0)
    dd = call(
        self_second_body, (f1, qs, ks, vs, ot1, log1, seg, self_out, *dsa), [((3, N, D), bf16)],
        specs=half_specs(1) + [VMEM] * 3, grid=(1,), name="self_bwd_b", us=7)[0]
    dd, gp = ob((dd, gp))
    ordered(big, dd)
    s = advance(big)
    keep, send = call(self_weights_body, (at, gate(dd, s), xx.reshape(N, D), vec2, vec3, db1), [((h3, D), bf16), ((h3, D), bf16)],
                      specs=[SMEM] + [VMEM] * 5, name="self_weights", us=4)
    got = core_swap(send, ns)
    rest = [Chain(dims, core, (keep2, got2, keep, got), h2 + h3, levels(yzx, xyz))]
    last = advance(rest)
    tp = call(target_grad_body, (at, gate(g1, last), self_qkv, dd), piece, [flat], specs=[SMEM] + [VMEM] * 3, name="target_grad", us=3)
    tp = exchange_out(tp, ns)
    last = (last, tp[0])
    for what in ("big", "rest", "big", "near", "rest", "halves", "big", "rest", "target", "big", "rest", "rest", "big", "rest", "ffn", "rest", "rest"):
        if what == "big" and not big[0].done:
            ordered(big, last)
            last = (last, advance(big))
            if big[0].done:
                other_half = core_swap(gate(big[0].own, last), ns)
        elif what == "rest" and not rest[0].done:
            ordered(rest, last)
            last = (last, advance(rest))
        elif what == "near":
            last = (last, tp[1], tp[2])
        elif what == "halves":
            result, mgrad = assemble(at, gate(rp, last)), assemble(at, gate(gp, last))
            last = (last, result, mgrad, tp[3])
        elif what == "target":
            tgrad = assemble(at, gate(tp, last))
            last = (last, tgrad)
        elif what == "ffn":
            while not big[0].done:
                advance(big)
                other_half = core_swap(big[0].own, ns)
            gw = call(final_ffn_body, (at, big[0].own, gate(other_half, last)), [((D, FF), f32), ((FF, D), f32), ((D, D), f32)],
                      specs=[SMEM] + [VMEM] * 2, name="final_ffn", us=5)
            last = (last, gw)
    while not rest[0].done:
        advance(rest)
    gw1, gw2, gwo2 = gw
    gcw, gwo1, gsw, dsb, dcb, gg, gb, gb1, gb2 = call(
        final_rest_body, (at, rest[0].own, core_swap(rest[0].own, ns)),
        [((3, D, D), f32), ((D, D), f32), ((3, D, D), f32)] + [((3, D), f32)] * 4 + [((FF // D, D), f32), ((1, D), f32)], [((32, D), f32)],
        specs=[SMEM, VMEM, VMEM], name="final_rest", us=3)
    return result, tgrad, mgrad, gsw, dsb, gwo1, gcw, dcb, gwo2, gw1, gb1.reshape(FF), gw2, gb2.reshape(D), gg, gb


def solution(mesh):
    from jax.sharding import PartitionSpec as P

    act, seg, rep = P("dp", "seq", None), P("dp", "seq"), P()
    return jax.shard_map(
        functools.partial(local, dict(mesh.shape)),
        mesh=mesh,
        in_specs=(act, act, seg, seg) + (rep,) * 12 + (act,),
        out_specs=(act, act, act) + (rep,) * 12,
        check_vma=False,
    )
```
